256 devices in a mesh: dp: 16 (over z_hi, y), tensor: 16 (over z_lo, x, core).
Axes of the slice: x: 4, y: 4, z: 8 (z_hi: 4, z_lo: 2; z = z_hi * 2 + z_lo), core: 2. Of those that a mesh axis runs over, the one named last changes fastest.
Arguments:
- layer_input: bfloat16 [16, 2, 256, 4096], P('dp', None, None, 'tensor'), may hold values from -6 to 6
- out_grad: bfloat16 [16, 2, 256, 4096], P('dp', None, None, 'tensor'), may hold values from -0.625 to 0.625
- norm_gain: float32 [4096], replicated, may hold values from 0.25 to 1.75
- gate_weight: bfloat16 [4096, 14336], P('dp', 'tensor'), may hold values from -0.09375 to 0.09375
- up_weight: bfloat16 [4096, 14336], P('dp', 'tensor'), may hold values from -0.09375 to 0.09375
- down_weight: bfloat16 [14336, 4096], P('tensor', 'dp'), may hold values from -0.046875 to 0.046875
- lengths: int32 [16, 2], P('dp'), may hold values from 1 to 256, as said below
- proj_in: bfloat16 [4096, 64], replicated, may hold values from -0.09375 to 0.09375
- proj_out: bfloat16 [14336, 64], P('tensor'), may hold values from -0.046875 to 0.046875
- queries: bfloat16 [4096, 4096], P('tensor', 'dp'), may hold values from -0.09375 to 0.09375
Outputs:
- grad_proj: float32 [16, 64, 64], P('dp')
- scores: float32 [16, 4096], P('dp', 'tensor')
The draws below stay inside these ranges and needn't reach their ends.
Inputs may be any that keep to these rules, and one draw needn't show every extreme that they name: `lengths`: each side of a pair has between 1 and 256 valid tokens, always from position 0; the chosen side of the first pair is full.
All inputs are finite; a program needn't handle non-finite values.
Results may differ from the reference program's by a relative error of at most 0.006.
Values may be sent and summed in bfloat16 or wider, within the bound.
A program may use at most 128 MiB of HBM per device.

```python
import jax
import jax.numpy as jnp
from jax import lax

D = 4096
FF = 14336
RANK = 64
SEQ = 256
PAIRS = 16
QUERIES = 4096


def draw_lengths(key, part):
    key = jax.random.fold_in(key, 7)
    drawn = jax.random.randint(key, (PAIRS, 2), 1, SEQ + 1, dtype=jnp.int32)
    return drawn.at[0, 0].set(SEQ)


def block_levels(own_key, dims, split, low, largest):
    def one(axis_at, blocks):
        draws = jax.random.uniform(jax.random.fold_in(jax.random.fold_in(own_key, 6), axis_at), (blocks,), jnp.float32, low / len(split), largest / len(split))
        return jnp.repeat(jnp.exp(draws), dims[axis_at] // blocks).reshape((-1,) + (1,) * (len(dims) - axis_at - 1))

    factor_of = one(*split[0])
    for cut in split[1:]:
        factor_of = factor_of * one(*cut)
    return factor_of


def noise(own_key, dims, spread, bound, cuts=(), kind=jnp.bfloat16):
    result = spread * jax.random.normal(own_key, dims, jnp.float32)
    if cuts:
        result = result * block_levels(own_key, dims, cuts, -0.22, 0.18)
    return jnp.clip(result, -bound, bound).astype(kind)


def setup_inputs(seed: int = 0) -> dict:
    arg_keys = jax.random.split(jax.random.key(seed), 11)
    layer_input = noise(arg_keys[0], (PAIRS, 2, SEQ, D), 1.0, 6.0, ((0, 16), (3, 16)))
    out_grad = noise(arg_keys[1], (PAIRS, 2, SEQ, D), ((2 * SEQ) ** -0.5), 0.625, ((0, 16), (3, 16)))
    norm_gain = jnp.clip(1.0 + 0.15 * jax.random.normal(arg_keys[2], (D,), jnp.float32), 0.25, 1.75)
    gate_weight = noise(arg_keys[3], (D, FF), D ** -0.5, 0.09375, ((0, 16), (1, 16)))
    up_weight = noise(arg_keys[4], (D, FF), D ** -0.5, 0.09375, ((0, 16), (1, 16)))
    down_weight = noise(arg_keys[5], (FF, D), FF ** -0.5, 0.046875, ((0, 16), (1, 16)))
    lengths = draw_lengths(jax.random.fold_in(arg_keys[10], 71), 0)
    proj_in = noise(arg_keys[7], (D, RANK), D ** -0.5, 0.09375)
    proj_out = noise(arg_keys[8], (FF, RANK), FF ** -0.5, 0.046875, ((0, 16),))
    queries = noise(arg_keys[9], (QUERIES, RANK * RANK), (RANK * RANK) ** -0.5, 0.09375, ((0, 16), (1, 16)))
    return dict(layer_input=layer_input, out_grad=out_grad, norm_gain=norm_gain, gate_weight=gate_weight, up_weight=up_weight, down_weight=down_weight, lengths=lengths, proj_in=proj_in, proj_out=proj_out, queries=queries)


def reference(layer_input, out_grad, norm_gain, gate_weight, up_weight, down_weight, lengths, proj_in, proj_out, queries):
    positions = jnp.arange(SEQ, dtype=jnp.int32)

    def one_pair(items):
        inputs, grads_in, lens = items
        values = inputs.reshape(2 * SEQ, D).astype(jnp.float32)
        factor = lax.rsqrt(lax.optimization_barrier(jnp.mean(values * values, axis=1, keepdims=True)) + 1e-05)
        normed = (values * factor * norm_gain.astype(jnp.float32)).astype(jnp.bfloat16)
        grads = grads_in.reshape(2 * SEQ, D)
        gate = jnp.dot(normed, gate_weight, preferred_element_type=jnp.float32)
        up = jnp.dot(normed, up_weight, preferred_element_type=jnp.float32)
        back = jnp.dot(grads, down_weight.T, preferred_element_type=jnp.float32)
        sig = jax.nn.sigmoid(gate)
        dgate = (back * up * sig * (1.0 + gate * (1.0 - sig))).astype(jnp.bfloat16)
        right = jnp.dot(dgate, proj_out, preferred_element_type=jnp.float32)
        left = jnp.dot(normed, proj_in, preferred_element_type=jnp.float32)
        mask = (positions[None, :] < lens[:, None]).astype(jnp.float32).reshape(2 * SEQ)
        return jnp.einsum('tr,ts->rs', left * mask[:, None], right, precision=lax.Precision.HIGHEST)
    grad_proj = lax.map(one_pair, (layer_input, out_grad, lengths))
    flat = grad_proj.reshape(PAIRS, RANK * RANK).astype(jnp.bfloat16)
    scores = jnp.dot(flat, queries.T, preferred_element_type=jnp.float32)
    return (grad_proj, scores)
```

```python
import jax
import jax.numpy as jnp
from jax import lax
from jax.experimental import pallas as pl
from jax.experimental.pallas import tpu as pltpu
from jax.sharding import PartitionSpec as P

MESH = pl.DeviceIdType.MESH
F32 = jnp.float32
BF16 = jnp.bfloat16
TOK = 512
KB = 256
NB = 16
HID = 896
RANK = 64


def mod(a, n):
    return lax.rem(a + 2 * n, n)


def coords():
    dp = lax.axis_index("dp")
    t = lax.axis_index("tensor")
    z_hi, y = dp // 4, lax.rem(dp, 4)
    z_lo, x, c = t // 8, lax.rem(t // 2, 4), lax.rem(t, 2)
    return x, y, 2 * z_hi + z_lo, c


def device(x, y, z, c):
    return ((z // 2) * 4 + y, lax.rem(z, 2) * 8 + x * 2 + c)


def gather_kernel(
    li, og, wg, wu, wd, po, pin, gain,
    out,
    tok, bwg, bwu, bwd, bpo, acc_g, acc_u, acc_b, acc_l, acc_s,
    r_tok, r_w, r_po, s_zw, s_zt, s_po, s_wz, s_wy, s_wc, s_tz, s_tx,
):
    x, y, z, c = coords()
    z_hi, z_lo = z // 2, lax.rem(z, 2)
    xp, xm, yp, ym = mod(x + 1, 4), mod(x - 1, 4), mod(y + 1, 4), mod(y - 1, 4)
    other = (x, y, z, 1 - c)
    ka, kc = lax.rem(z_hi, 2), z_hi // 2

    barrier = pltpu.get_barrier_semaphore()
    peers = [(xp, y, z, c), (xm, y, z, c), (x, yp, z, c), (x, ym, z, c), other]
    for dz in range(1, 8):
        for cc in (0, 1):
            peers.append((x, y, mod(z + dz, 8), cc))
    for p in peers:
        pl.semaphore_signal(barrier, inc=1, device_id=device(*p), device_id_type=MESH)
    pl.semaphore_wait(barrier, len(peers))

    waits = []

    def send(src, dst, ssem, rsem, to, cond=None):
        d = pltpu.make_async_remote_copy(
            src_ref=src, dst_ref=dst, send_sem=ssem, recv_sem=rsem,
            device_id=device(*to), device_id_type=MESH,
        )
        if cond is None:
            d.start()
            waits.append(d.wait_send)
        else:
            pl.when(cond)(lambda: d.start())
            waits.append(lambda: pl.when(cond)(lambda: d.wait_send()))

    halves = [(0, 0), (1, 0), (2, 0), (0, 1), (1, 1), (2, 1)]
    bufs = (bwg, bwu, bwd)

    def wslot(j, q):
        m, h = halves[q]
        n = KB // 2 if m < 2 else HID // 2
        return bufs[m].at[j, pl.ds(h * n, n)]

    def wsrc(q):
        m, h = halves[q]
        n = KB // 2 if m < 2 else HID // 2
        return (wg, wu, wd)[m].at[pl.ds(h * n, n)]

    def wwait(j, q):
        pltpu.make_async_copy(wslot(j, q), wslot(j, q), r_w.at[j, q]).wait()

    def twait(a, j):
        pltpu.make_async_copy(tok.at[a, j], tok.at[a, j], r_tok.at[a, j]).wait()

    kt = z_lo + 2 * c
    rel = mod(z_hi - kt, 4)
    f = lax.rem(z_hi, 2)
    jw = z_hi * 4 + y
    mine = rel == 0
    entry = jnp.where(rel == 1, 1, jnp.where(rel == 3, 0, 1 - z_lo))
    far_z = jnp.where(mine, mod(z + 1 - 2 * z_lo, 8), 2 * kt + entry)
    for q in range(6):
        send(wsrc(q), wslot(jw, q), s_zw.at[0, q], r_w.at[jw, q], (x, y, far_z, f))
    for q in range(6):
        send(wsrc(q), wslot(jw, q), s_zw.at[1, q], r_w.at[jw, q], other, mine & (f != c))

        def local(q=q):
            pltpu.make_async_copy(wsrc(q), wslot(jw, q), r_w.at[jw, q]).start()

        pl.when(mine & (f == c))(local)
    has_po = (z_lo == ka) & (c == kc)
    z1 = mod(z + 1 - 2 * z_lo, 8)
    send(po, bpo, s_po.at[0], r_po, other, has_po)
    send(po, bpo, s_po.at[1], r_po, (x, y, z1, 0), has_po)
    send(po, bpo, s_po.at[2], r_po, (x, y, z1, 1), has_po)
    pl.when(has_po)(lambda: pltpu.make_async_copy(po, bpo, r_po).start())

    b = lax.rem(z_hi, 2)
    i = z_hi // 2
    jt = z_lo * 8 + x * 2 + c
    aligned = z_lo == b
    step = jnp.where(aligned, 2, 1)
    for a in range(2):
        src = (li, og)[a]
        send(src, tok.at[a, jt], s_zt.at[0, a], r_tok.at[a, jt], (x, y, mod(z + step, 8), i))
        send(src, tok.at[a, jt], s_zt.at[1, a], r_tok.at[a, jt], (x, y, mod(z - step, 8), i))
        send(src, tok.at[a, jt], s_zt.at[2, a], r_tok.at[a, jt], other, aligned & (i != c))

        def local_t(src=src, a=a):
            pltpu.make_async_copy(src, tok.at[a, jt], r_tok.at[a, jt]).start()

        pl.when(aligned & (i == c))(local_t)

    s0 = lax.rem(c + z_hi, 2)
    zs = (mod(z_hi + s0, 4), mod(z_hi + s0 + 2, 4))

    def w_own(n):
        zz = zs[n]
        j = zz * 4 + y
        r = mod(zz - z_hi, 4)
        ent = jnp.where(r == 1, 1, jnp.where(r == 3, 0, 1 - ka))
        fwd = (r != 0) & (z_lo == ent)
        for q in range(6):
            wwait(j, q)
            send(wslot(j, q), wslot(j, q), s_wy.at[n, 0, q], r_w.at[j, q], (x, yp, z, c))
            send(wslot(j, q), wslot(j, q), s_wy.at[n, 1, q], r_w.at[j, q], (x, ym, z, c))
            send(wslot(j, q), wslot(j, q), s_wz.at[n, q], r_w.at[j, q], (x, y, z1, c), fwd)
            send(wslot(j, q), wslot(j, q), s_wc.at[n, 0, q], r_w.at[j, q], other)

    def w_next(n):
        zz = zs[n]
        jm, jp = zz * 4 + ym, zz * 4 + yp
        for q in range(6):
            for way, j, to in ((0, jm, yp), (1, jp, ym)):
                wwait(j, q)
                if q // 3 == way:
                    send(wslot(j, q), wslot(j, q), s_wy.at[n, way, 6 + q % 3], r_w.at[j, q], (x, to, z, c))
                send(wslot(j, q), wslot(j, q), s_wc.at[n, 1 + way, q], r_w.at[j, q], other)

    def w_last(n):
        j = zs[n] * 4 + mod(y + 2, 4)
        for q in range(6):
            wwait(j, q)
            send(wslot(j, q), wslot(j, q), s_wc.at[n, 3, q], r_w.at[j, q], other)

    r0 = mod(z - 2 * z_lo - 4 * c, 8)
    u0 = 1 - mod(r0 + 7, 8) // 4
    us = (u0, 1 - u0)

    def t_own(n):
        u = us[n]
        r = mod(r0 - u, 8)
        for cc in (0, 1):
            j = u * 8 + x * 2 + cc
            for a in (0, 1):
                twait(a, j)
                blk = tok.at[a, j]
                send(blk, blk, s_tx.at[n, cc, 0, a], r_tok.at[a, j], (xp, y, z, c))
                send(blk, blk, s_tx.at[n, cc, 1, a], r_tok.at[a, j], (xm, y, z, c))
                up = (r == 1) | (r == 2) if a == 0 else r == 1
                down = (r == 7) | (r == 6) if a == 1 else r == 7
                send(blk, blk, s_tz.at[n, cc, 0, a], r_tok.at[a, j], (x, y, mod(z + 2, 8), c), up)
                send(blk, blk, s_tz.at[n, cc, 1, a], r_tok.at[a, j], (x, y, mod(z - 2, 8), c), down)

    def t_next(n):
        u = us[n]
        for cc in (0, 1):
            jm, jp = u * 8 + xm * 2 + cc, u * 8 + xp * 2 + cc
            twait(0, jm)
            send(tok.at[0, jm], tok.at[0, jm], s_tx.at[n, cc, 0, 2], r_tok.at[0, jm], (xp, y, z, c))
            twait(1, jp)
            send(tok.at[1, jp], tok.at[1, jp], s_tx.at[n, cc, 1, 2], r_tok.at[1, jp], (xm, y, z, c))
            twait(1, jm)
            twait(0, jp)

    def t_last(n):
        for cc in (0, 1):
            j = us[n] * 8 + mod(x + 2, 4) * 2 + cc
            twait(0, j)
            twait(1, j)

    w_own(0)
    t_own(0)
    t_own(1)
    w_next(0)
    t_next(0)
    w_own(1)
    t_next(1)
    w_next(1)
    t_last(0)
    t_last(1)
    w_last(0)
    w_last(1)
    for n in range(2):
        zz = mod(zs[n] + 1, 4)
        for dy in range(4):
            j = zz * 4 + mod(y + dy, 4)
            for q in range(6):
                wwait(j, q)
    pltpu.make_async_copy(bpo, bpo, r_po).wait()
    for w in waits:
        w()

    for ref in (acc_g, acc_u, acc_b, acc_l, acc_s):
        ref[...] = jnp.zeros_like(ref)

    @pl.loop(0, NB)
    def _(j):
        v = tok[0, j].astype(F32)
        acc_s[...] += jnp.broadcast_to(jnp.sum(v * v, axis=1, keepdims=True), acc_s.shape)
        n = (v * gain[j]).astype(BF16)
        acc_g[...] += jnp.dot(n, bwg[j], preferred_element_type=F32)
        acc_u[...] += jnp.dot(n, bwu[j], preferred_element_type=F32)
        acc_l[...] += jnp.dot(n, pin[j], preferred_element_type=F32)
        acc_b[...] += lax.dot_general(
            tok[1, j], bwd[j], (((1,), (1,)), ((), ())), preferred_element_type=F32
        )

    out[...] = jnp.zeros_like(out)

    @pl.loop(0, TOK // 128)
    def _(t):
        rows = pl.ds(pl.multiple_of(t * 128, 128), 128)
        factor = lax.rsqrt(acc_s[rows, 0:1] * (1.0 / 4096.0) + 1e-05)
        gate = acc_g[rows, :] * factor
        up = acc_u[rows, :] * factor
        sig = 1.0 / (1.0 + jnp.exp(-gate))
        dgate = (acc_b[rows, :] * up * sig * (1.0 + gate * (1.0 - sig))).astype(BF16)
        right = jnp.dot(dgate, bpo[...], preferred_element_type=F32)
        left = acc_l[rows, :] * factor
        out[...] += lax.dot_general(
            left, right, (((0,), (0,)), ((), ())),
            precision=lax.Precision.HIGHEST, preferred_element_type=F32,
        )


def gathered(li, og, wg, wu, wd, po, pin, gain):
    any_ = pl.BlockSpec(memory_space=pl.ANY)
    vmem = pl.BlockSpec(memory_space=pltpu.VMEM)
    dma = pltpu.SemaphoreType.DMA
    return pl.pallas_call(
        gather_kernel,
        out_shape=jax.ShapeDtypeStruct((RANK, RANK), F32),
        in_specs=[any_] * 6 + [vmem] * 2,
        out_specs=vmem,
        scratch_shapes=[
            pltpu.VMEM((2, NB, TOK, KB), BF16),
            pltpu.VMEM((NB, KB, HID), BF16),
            pltpu.VMEM((NB, KB, HID), BF16),
            pltpu.VMEM((NB, HID, KB), BF16),
            pltpu.VMEM((HID, RANK), BF16),
            pltpu.VMEM((TOK, HID), F32),
            pltpu.VMEM((TOK, HID), F32),
            pltpu.VMEM((TOK, HID), F32),
            pltpu.VMEM((TOK, RANK), F32),
            pltpu.VMEM((TOK, 128), F32),
            dma((2, NB)),
            dma((NB, 6)),
            dma,
            dma((2, 6)),
            dma((3, 2)),
            dma((3,)),
            dma((2, 6)),
            dma((2, 2, 9)),
            dma((2, 4, 6)),
            dma((2, 2, 2, 2)),
            dma((2, 2, 2, 3)),
        ],
        compiler_params=pltpu.CompilerParams(
            collective_id=0, has_side_effects=True, vmem_limit_bytes=60 << 20
        ),
    )(li, og, wg, wu, wd, po, pin, gain)


def on_device(
    layer_input,
    out_grad,
    norm_gain,
    gate_weight,
    up_weight,
    down_weight,
    lengths,
    proj_in,
    proj_out,
    queries,
):
    seq = layer_input.shape[2]
    positions = jnp.arange(seq, dtype=jnp.int32)
    valid = positions[None, None, :] < lengths[:, :, None]
    grads = jnp.where(valid[..., None], out_grad, jnp.zeros_like(out_grad))
    part = gathered(
        layer_input.reshape(TOK, KB),
        grads.reshape(TOK, KB),
        gate_weight,
        up_weight,
        down_weight,
        proj_out,
        proj_in.reshape(NB, KB, RANK),
        norm_gain.reshape(NB, 1, KB),
    )
    _, y, z, c = coords()
    dp = lax.axis_index("dp")
    pair = (lax.rem(z, 2) + 2 * c) * 4 + y
    every = jnp.where(jnp.arange(16)[:, None, None] == pair, part[None], 0.0)
    every = lax.psum(every, ("dp", "tensor"))
    grad_proj = lax.dynamic_slice_in_dim(every, dp, 1, 0)
    flat = every.reshape(16, RANK * RANK).astype(BF16)
    block = lax.dynamic_slice_in_dim(flat, dp * KB, KB, 1)
    scores = lax.dot_general(
        block, queries, (((1,), (1,)), ((), ())), preferred_element_type=F32
    )
    scores = lax.psum_scatter(scores, "dp", scatter_dimension=0, tiled=True)
    return (grad_proj, scores)


def solution(mesh):
    in_specs = (
        P("dp", None, None, "tensor"),
        P("dp", None, None, "tensor"),
        P(),
        P("dp", "tensor"),
        P("dp", "tensor"),
        P("tensor", "dp"),
        P("dp", None),
        P(),
        P("tensor", None),
        P("tensor", "dp"),
    )
    out_specs = (P("dp", None, None), P("dp", "tensor"))
    return jax.shard_map(
        on_device, mesh=mesh, in_specs=in_specs, out_specs=out_specs, check_vma=False
    )
```

```python
import jax
import jax.numpy as jnp
from jax import lax
from jax.experimental import pallas as pl
from jax.experimental.pallas import tpu as pltpu
from jax.sharding import PartitionSpec as P

MESH = pl.DeviceIdType.MESH
F32 = jnp.float32
BF16 = jnp.bfloat16
TOK = 512
KB = 256
NB = 16
HID = 896
RANK = 64


def mod(a, n):
    return lax.rem(a + 2 * n, n)


def coords():
    dp = lax.axis_index("dp")
    t = lax.axis_index("tensor")
    z_hi, y = dp // 4, lax.rem(dp, 4)
    z_lo, x, c = t // 8, lax.rem(t // 2, 4), lax.rem(t, 2)
    return x, y, 2 * z_hi + z_lo, c


def device(x, y, z, c):
    return ((z // 2) * 4 + y, lax.rem(z, 2) * 8 + x * 2 + c)


def gather_kernel(
    li, og, wg, wu, wd, po, pin, gain,
    out,
    tok, bwg, bwu, bwd, bpo, acc_g, acc_u, acc_b, acc_l, acc_s, acc_o,
    r_tok, r_w, r_po, s_zw, s_zt, s_po, s_wz, s_wy, s_wc, s_tz, s_tx,
):
    x, y, z, c = coords()
    z_hi, z_lo = z // 2, lax.rem(z, 2)
    xp, xm, yp, ym = mod(x + 1, 4), mod(x - 1, 4), mod(y + 1, 4), mod(y - 1, 4)
    other = (x, y, z, 1 - c)
    ka, kc = lax.rem(z_hi, 2), z_hi // 2

    barrier = pltpu.get_barrier_semaphore()
    peers = [(xp, y, z, c), (xm, y, z, c), (x, yp, z, c), (x, ym, z, c), other]
    for dz in range(1, 8):
        for cc in (0, 1):
            peers.append((x, y, mod(z + dz, 8), cc))
    for p in peers:
        pl.semaphore_signal(barrier, inc=1, device_id=device(*p), device_id_type=MESH)
    pl.semaphore_wait(barrier, len(peers))

    waits = []

    def send(src, dst, ssem, rsem, to, cond=None):
        d = pltpu.make_async_remote_copy(
            src_ref=src, dst_ref=dst, send_sem=ssem, recv_sem=rsem,
            device_id=device(*to), device_id_type=MESH,
        )
        if cond is None:
            d.start()
            waits.append(d.wait_send)
        else:
            pl.when(cond)(lambda: d.start())
            waits.append(lambda: pl.when(cond)(lambda: d.wait_send()))

    halves = [(0, 0), (1, 0), (2, 0), (0, 1), (1, 1), (2, 1)]
    bufs = (bwg, bwu, bwd)

    def wslot(j, q):
        m, h = halves[q]
        n = KB // 2 if m < 2 else HID // 2
        return bufs[m].at[j, pl.ds(h * n, n)]

    def wsrc(q):
        m, h = halves[q]
        n = KB // 2 if m < 2 else HID // 2
        return (wg, wu, wd)[m].at[pl.ds(h * n, n)]

    def wwait(j, q):
        pltpu.make_async_copy(wslot(j, q), wslot(j, q), r_w.at[j, q]).wait()

    def twait(a, j):
        pltpu.make_async_copy(tok.at[a, j], tok.at[a, j], r_tok.at[a, j]).wait()

    kt = z_lo + 2 * c
    rel = mod(z_hi - kt, 4)
    f = lax.rem(z_hi, 2)
    jw = z_hi * 4 + y
    mine = rel == 0
    entry = jnp.where(rel == 1, 1, jnp.where(rel == 3, 0, 1 - z_lo))
    far_z = jnp.where(mine, mod(z + 1 - 2 * z_lo, 8), 2 * kt + entry)
    for q in range(6):
        send(wsrc(q), wslot(jw, q), s_zw.at[0, q], r_w.at[jw, q], (x, y, far_z, f))
    for q in range(6):
        send(wsrc(q), wslot(jw, q), s_zw.at[1, q], r_w.at[jw, q], other, mine & (f != c))

        def local(q=q):
            pltpu.make_async_copy(wsrc(q), wslot(jw, q), r_w.at[jw, q]).start()

        pl.when(mine & (f == c))(local)
    has_po = (z_lo == ka) & (c == kc)
    z1 = mod(z + 1 - 2 * z_lo, 8)
    send(po, bpo, s_po.at[0], r_po, other, has_po)
    send(po, bpo, s_po.at[1], r_po, (x, y, z1, 0), has_po)
    send(po, bpo, s_po.at[2], r_po, (x, y, z1, 1), has_po)
    pl.when(has_po)(lambda: pltpu.make_async_copy(po, bpo, r_po).start())

    b = lax.rem(z_hi, 2)
    i = z_hi // 2
    jt = z_lo * 8 + x * 2 + c
    aligned = z_lo == b
    step = jnp.where(aligned, 2, 1)
    for a in range(2):
        src = (li, og)[a]
        send(src, tok.at[a, jt], s_zt.at[0, a], r_tok.at[a, jt], (x, y, mod(z + step, 8), i))
        send(src, tok.at[a, jt], s_zt.at[1, a], r_tok.at[a, jt], (x, y, mod(z - step, 8), i))
        send(src, tok.at[a, jt], s_zt.at[2, a], r_tok.at[a, jt], other, aligned & (i != c))

        def local_t(src=src, a=a):
            pltpu.make_async_copy(src, tok.at[a, jt], r_tok.at[a, jt]).start()

        pl.when(aligned & (i == c))(local_t)

    s0 = lax.rem(c + z_hi, 2)
    zs = (mod(z_hi + s0, 4), mod(z_hi + s0 + 2, 4))

    def w_own(n):
        zz = zs[n]
        j = zz * 4 + y
        r = mod(zz - z_hi, 4)
        ent = jnp.where(r == 1, 1, jnp.where(r == 3, 0, 1 - ka))
        fwd = (r != 0) & (z_lo == ent)
        for q in range(6):
            wwait(j, q)
            send(wslot(j, q), wslot(j, q), s_wy.at[n, 0, q], r_w.at[j, q], (x, yp, z, c))
            send(wslot(j, q), wslot(j, q), s_wy.at[n, 1, q], r_w.at[j, q], (x, ym, z, c))
            send(wslot(j, q), wslot(j, q), s_wz.at[n, q], r_w.at[j, q], (x, y, z1, c), fwd)
            send(wslot(j, q), wslot(j, q), s_wc.at[n, 0, q], r_w.at[j, q], other)

    def w_next(n):
        zz = zs[n]
        jm, jp = zz * 4 + ym, zz * 4 + yp
        for q in range(6):
            for way, j, to in ((0, jm, yp), (1, jp, ym)):
                wwait(j, q)
                if q // 3 == way:
                    send(wslot(j, q), wslot(j, q), s_wy.at[n, way, 6 + q % 3], r_w.at[j, q], (x, to, z, c))
                send(wslot(j, q), wslot(j, q), s_wc.at[n, 1 + way, q], r_w.at[j, q], other)

    def w_last(n):
        j = zs[n] * 4 + mod(y + 2, 4)
        for q in range(6):
            wwait(j, q)
            send(wslot(j, q), wslot(j, q), s_wc.at[n, 3, q], r_w.at[j, q], other)

    r0 = mod(z - 2 * z_lo - 4 * c, 8)
    u0 = 1 - mod(r0 + 7, 8) // 4
    us = (u0, 1 - u0)

    def t_own(n):
        u = us[n]
        r = mod(r0 - u, 8)
        for cc in (0, 1):
            j = u * 8 + x * 2 + cc
            for a in (0, 1):
                twait(a, j)
                blk = tok.at[a, j]
                send(blk, blk, s_tx.at[n, cc, 0, a], r_tok.at[a, j], (xp, y, z, c))
                send(blk, blk, s_tx.at[n, cc, 1, a], r_tok.at[a, j], (xm, y, z, c))
                up = (r == 1) | (r == 2) if a == 0 else r == 1
                down = (r == 7) | (r == 6) if a == 1 else r == 7
                send(blk, blk, s_tz.at[n, cc, 0, a], r_tok.at[a, j], (x, y, mod(z + 2, 8), c), up)
                send(blk, blk, s_tz.at[n, cc, 1, a], r_tok.at[a, j], (x, y, mod(z - 2, 8), c), down)

    def t_next(n):
        u = us[n]
        for cc in (0, 1):
            jm, jp = u * 8 + xm * 2 + cc, u * 8 + xp * 2 + cc
            twait(0, jm)
            send(tok.at[0, jm], tok.at[0, jm], s_tx.at[n, cc, 0, 2], r_tok.at[0, jm], (xp, y, z, c))
            twait(1, jp)
            send(tok.at[1, jp], tok.at[1, jp], s_tx.at[n, cc, 1, 2], r_tok.at[1, jp], (xm, y, z, c))
            twait(1, jm)
            twait(0, jp)

    def t_last(n):
        for cc in (0, 1):
            j = us[n] * 8 + mod(x + 2, 4) * 2 + cc
            twait(0, j)
            twait(1, j)

    w_own(0)
    t_own(0)
    t_own(1)
    w_next(0)
    t_next(0)
    w_own(1)
    t_next(1)
    w_next(1)
    t_last(0)
    t_last(1)
    w_last(0)
    w_last(1)
    for n in range(2):
        zz = mod(zs[n] + 1, 4)
        for dy in range(4):
            j = zz * 4 + mod(y + dy, 4)
            for q in range(6):
                wwait(j, q)
    pltpu.make_async_copy(bpo, bpo, r_po).wait()
    for w in waits:
        w()

    for ref in (acc_g, acc_u, acc_b, acc_l, acc_s):
        ref[...] = jnp.zeros_like(ref)

    @pl.loop(0, NB)
    def _(j):
        v = tok[0, j].astype(F32)
        v = v * v
        acc_s[...] += v[:, :128] + v[:, 128:]

    mean = jnp.sum(acc_s[...], axis=1, keepdims=True) * (1.0 / 4096.0)
    acc_s[...] = jnp.broadcast_to(lax.rsqrt(mean + 1e-05), acc_s.shape)

    @pl.loop(0, NB)
    def _(j):
        n = (tok[0, j].astype(F32) * acc_s[:, 0:1] * gain[j]).astype(BF16)
        acc_g[...] += jnp.dot(n, bwg[j], preferred_element_type=F32)
        acc_u[...] += jnp.dot(n, bwu[j], preferred_element_type=F32)
        acc_l[...] += jnp.dot(n, pin[j], preferred_element_type=F32)
        acc_b[...] += lax.dot_general(
            tok[1, j], bwd[j], (((1,), (1,)), ((), ())), preferred_element_type=F32
        )

    acc_o[...] = jnp.zeros_like(acc_o)

    @pl.loop(0, TOK // 128)
    def _(t):
        rows = pl.ds(pl.multiple_of(t * 128, 128), 128)
        gate = acc_g[rows, :]
        sig = 1.0 / (1.0 + jnp.exp(-gate))
        dgate = (acc_b[rows, :] * acc_u[rows, :] * sig * (1.0 + gate * (1.0 - sig))).astype(BF16)
        right = jnp.dot(dgate, bpo[...], preferred_element_type=F32)
        acc_o[...] += lax.dot_general(
            acc_l[rows, :], right, (((0,), (0,)), ((), ())),
            precision=lax.Precision.HIGHEST, preferred_element_type=F32,
        )

    for j in range(NB):
        out[j] = acc_o[4 * j:4 * j + 4, :]


def finish_kernel(part, q, grad, score, got1, mine, got2, got3, got4, rows, r1, r2, r3, r4, s1, s2, s3, s4):
    x, y, z, c = coords()
    z_hi, z_lo = z // 2, lax.rem(z, 2)
    ph = z_lo + 2 * c
    piece = z_hi * 4 + x

    def dev2(zh, yy, zl, xx, cc):
        return (zh * 4 + yy, zl * 8 + xx * 2 + cc)

    team = [(mod(z_hi + d // 4, 4), mod(x + d % 4, 4)) for d in range(1, 16)]
    same_t = [(mod(z_hi + d // 4, 4), mod(y + d % 4, 4)) for d in range(1, 16)]
    every_t = [(lax.rem(z_lo + d // 8, 2), mod(x + (d // 2) % 4, 4), lax.rem(c + d % 2, 2)) for d in range(16)]
    barrier = pltpu.get_barrier_semaphore()

    def tell(to):
        pl.semaphore_signal(barrier, inc=1, device_id=to, device_id_type=MESH)

    for zh, xx in team:
        tell(dev2(zh, y, z_lo, xx, c))
    for zh, yy in same_t:
        tell(dev2(zh, yy, z_lo, x, c))
    for d in range(16):
        tell(dev2(d // 4, y, lax.rem(z_hi, 2), d % 4, z_hi // 2))
        tell(dev2(z_hi, d // 4, d % 2, y, (d // 2) % 2))
    pl.semaphore_wait(barrier, 62)
    waits = []

    def send(src, dst, ssem, rsem, to, self_=None):
        d = pltpu.make_async_remote_copy(
            src_ref=src, dst_ref=dst, send_sem=ssem, recv_sem=rsem, device_id=to, device_id_type=MESH,
        )
        if self_ is None:
            d.start()
            waits.append(d.wait_send)
        else:
            def stay():
                pltpu.make_async_copy(src, dst, rsem).start()

            pl.when(jnp.logical_not(self_))(lambda: d.start())
            pl.when(self_)(stay)
            waits.append(lambda: pl.when(jnp.logical_not(self_))(lambda: d.wait_send()))

    def arrived(ref, sem):
        pltpu.make_async_copy(ref, ref, sem).wait()

    for n, (zh, xx) in enumerate(team):
        send(part.at[zh * 4 + xx], got1.at[piece], s1.at[n], r1.at[piece], dev2(zh, y, z_lo, xx, c))
    total = part[piece]
    for zh, xx in team:
        m = zh * 4 + xx
        arrived(got1.at[m], r1.at[m])
        total = total + got1[m]
    mine[...] = total
    pair = ph * 4 + y
    for n, (zl, xx, cc) in enumerate(every_t):
        send(mine, got3.at[pair], s3.at[n], r3.at[pair], dev2(z_hi, x, zl, xx, cc), (x == y) if n == 0 else None)
    for n, (zl, xx, cc) in enumerate(every_t):
        send(mine, got2.at[piece], s2.at[n], r2.at[piece], dev2(ph, y, zl, xx, cc), (ph == z_hi) if n == 0 else None)
    for p in range(16):
        arrived(got3.at[p], r3.at[p])
    s = jnp.zeros((16, KB), F32)
    for r in range(4):
        f = got3[:, r, :].astype(BF16)
        s = s + lax.dot_general(
            f, q[:, r * RANK:(r + 1) * RANK], (((1,), (1,)), ((), ())), preferred_element_type=F32
        )
    for p in range(16):
        rows[p] = s[p:p + 1, :]
    me = z_hi * 4 + y
    for n, (zh, yy) in enumerate(same_t):
        send(rows.at[zh * 4 + yy], got4.at[me], s4.at[n], r4.at[me], dev2(zh, yy, z_lo, x, c))
    for p in range(16):
        arrived(got2.at[p], r2.at[p])
        grad[p] = got2[p]
    total = rows[me]
    for zh, yy in same_t:
        m = zh * 4 + yy
        arrived(got4.at[m], r4.at[m])
        total = total + got4[m]
    score[...] = total
    for w in waits:
        w()


def finish(part, queries):
    vmem = pl.BlockSpec(memory_space=pltpu.VMEM)
    dma = pltpu.SemaphoreType.DMA
    piece = pltpu.VMEM((NB, 4, RANK), F32)
    row = pltpu.VMEM((16, 1, KB), F32)
    return pl.pallas_call(
        finish_kernel,
        out_shape=(
            jax.ShapeDtypeStruct((NB, 4, RANK), F32),
            jax.ShapeDtypeStruct((1, KB), F32),
        ),
        in_specs=[vmem] * 2,
        out_specs=(vmem, vmem),
        scratch_shapes=[piece, pltpu.VMEM((4, RANK), F32), piece, piece, row, row]
        + [dma((16,))] * 8,
        compiler_params=pltpu.CompilerParams(collective_id=1, has_side_effects=True),
    )(part, queries)


def gathered(li, og, wg, wu, wd, po, pin, gain):
    any_ = pl.BlockSpec(memory_space=pl.ANY)
    vmem = pl.BlockSpec(memory_space=pltpu.VMEM)
    dma = pltpu.SemaphoreType.DMA
    return pl.pallas_call(
        gather_kernel,
        out_shape=jax.ShapeDtypeStruct((NB, 4, RANK), F32),
        in_specs=[any_] * 6 + [vmem] * 2,
        out_specs=vmem,
        scratch_shapes=[
            pltpu.VMEM((2, NB, TOK, KB), BF16),
            pltpu.VMEM((NB, KB, HID), BF16),
            pltpu.VMEM((NB, KB, HID), BF16),
            pltpu.VMEM((NB, HID, KB), BF16),
            pltpu.VMEM((HID, RANK), BF16),
            pltpu.VMEM((TOK, HID), F32),
            pltpu.VMEM((TOK, HID), F32),
            pltpu.VMEM((TOK, HID), F32),
            pltpu.VMEM((TOK, RANK), F32),
            pltpu.VMEM((TOK, 128), F32),
            pltpu.VMEM((RANK, RANK), F32),
            dma((2, NB)),
            dma((NB, 6)),
            dma,
            dma((2, 6)),
            dma((3, 2)),
            dma((3,)),
            dma((2, 6)),
            dma((2, 2, 9)),
            dma((2, 4, 6)),
            dma((2, 2, 2, 2)),
            dma((2, 2, 2, 3)),
        ],
        compiler_params=pltpu.CompilerParams(
            collective_id=0, has_side_effects=True, vmem_limit_bytes=60 << 20
        ),
    )(li, og, wg, wu, wd, po, pin, gain)


def on_device(
    layer_input,
    out_grad,
    norm_gain,
    gate_weight,
    up_weight,
    down_weight,
    lengths,
    proj_in,
    proj_out,
    queries,
):
    seq = layer_input.shape[2]
    positions = jnp.arange(seq, dtype=jnp.int32)
    valid = positions[None, None, :] < lengths[:, :, None]
    grads = jnp.where(valid[..., None], out_grad, jnp.zeros_like(out_grad))
    part = gathered(
        layer_input.reshape(TOK, KB),
        grads.reshape(TOK, KB),
        gate_weight,
        up_weight,
        down_weight,
        proj_out,
        proj_in.reshape(NB, KB, RANK),
        norm_gain.reshape(NB, 1, KB),
    )
    grad, scores = finish(part, queries)
    return (grad.reshape(1, RANK, RANK), scores)


def solution(mesh):
    in_specs = (
        P("dp", None, None, "tensor"),
        P("dp", None, None, "tensor"),
        P(),
        P("dp", "tensor"),
        P("dp", "tensor"),
        P("tensor", "dp"),
        P("dp", None),
        P(),
        P("tensor", None),
        P("tensor", "dp"),
    )
    out_specs = (P("dp", None, None), P("dp", "tensor"))
    return jax.shard_map(
        on_device, mesh=mesh, in_specs=in_specs, out_specs=out_specs, check_vma=False
    )
```

```python
import jax
import jax.numpy as jnp
from jax import lax
from jax.experimental import pallas as pl
from jax.experimental.pallas import tpu as pltpu
from jax.sharding import PartitionSpec as P

MESH = pl.DeviceIdType.MESH
F32 = jnp.float32
BF16 = jnp.bfloat16
TOK = 512
KB = 256
NB = 16
HID = 896
RANK = 64
NSEND = 176

ORDERS = (
    (
        0, 1, 2, 3, 4, 5, 8, 9, 10, 11, 12, 13, 28, 29, 30, 31, 6, 7, 22, 20, 23, 21, 32, 33,
        54, 24, 52, 34, 35, 55, 25, 53, 36, 37, 14, 38, 39, 56, 73, 57, 15, 60, 63, 72, 74, 61, 64, 41,
        62, 16, 26, 40, 65, 42, 43, 27, 58, 44, 45, 59, 17, 66, 75, 18, 47, 67, 49, 68, 69, 46, 19, 70,
        48, 51, 50, 71,
    ),
    (
        0, 1, 2, 3, 4, 5, 8, 6, 7, 9, 28, 29, 10, 30, 31, 11, 33, 60, 12, 32, 35, 37, 61, 13,
        34, 63, 14, 20, 27, 36, 64, 52, 24, 59, 39, 62, 38, 41, 21, 15, 65, 56, 40, 43, 16, 53, 42, 72,
        17, 45, 66, 47, 44, 18, 22, 25, 67, 69, 54, 19, 57, 23, 46, 49, 74, 26, 68, 51, 55, 48, 58, 70,
        50, 73, 75, 71,
    ),
    (
        0, 1, 2, 3, 4, 5, 8, 6, 7, 14, 28, 29, 9, 41, 15, 40, 22, 31, 26, 60, 10, 43, 54, 16,
        30, 33, 58, 23, 42, 27, 45, 11, 17, 66, 55, 35, 32, 59, 18, 12, 47, 44, 73, 20, 63, 19, 21, 61,
        75, 52, 13, 49, 67, 37, 53, 34, 24, 69, 72, 46, 56, 25, 51, 62, 39, 48, 57, 70, 36, 74, 64, 68,
        71, 50, 65, 38,
    ),
    (
        0, 1, 2, 3, 4, 5, 8, 6, 7, 28, 29, 9, 14, 60, 31, 22, 30, 10, 41, 54, 40, 33, 23, 11,
        61, 35, 32, 55, 12, 63, 66, 26, 13, 73, 37, 34, 58, 15, 39, 62, 27, 64, 36, 16, 59, 43, 38, 24,
        65, 20, 75, 42, 17, 45, 56, 44, 47, 25, 52, 67, 18, 21, 19, 69, 46, 57, 53, 49, 68, 74, 72, 51,
        48, 70, 50, 71,
    ),
    (
        0, 1, 2, 3, 4, 5, 8, 6, 7, 9, 28, 29, 22, 30, 31, 10, 54, 60, 33, 23, 61, 11, 26, 55,
        35, 32, 34, 63, 58, 12, 73, 27, 13, 62, 37, 20, 36, 59, 39, 21, 52, 38, 64, 14, 75, 65, 40, 53,
        41, 66, 24, 72, 15, 16, 56, 17, 42, 43, 25, 18, 19, 44, 45, 57, 47, 46, 49, 67, 51, 74, 48, 69,
        50, 70, 68, 71,
    ),
    (
        0, 1, 2, 3, 4, 5, 8, 6, 7, 14, 28, 29, 9, 15, 40, 41, 31, 22, 60, 10, 43, 16, 54, 30,
        33, 45, 42, 23, 11, 17, 66, 35, 55, 12, 26, 32, 47, 73, 18, 44, 13, 63, 58, 27, 61, 37, 67, 19,
        59, 69, 24, 20, 34, 49, 75, 46, 56, 39, 25, 21, 36, 52, 64, 62, 51, 48, 70, 57, 68, 53, 65, 38,
        74, 71, 50, 72,
    ),
    (
        0, 1, 2, 3, 4, 5, 8, 6, 7, 20, 21, 22, 23, 9, 14, 52, 28, 29, 53, 10, 24, 40, 41, 54,
        55, 11, 30, 31, 25, 72, 56, 12, 33, 60, 15, 73, 57, 32, 35, 13, 74, 37, 66, 26, 34, 43, 16, 61,
        63, 27, 58, 36, 39, 42, 64, 59, 45, 62, 17, 75, 38, 65, 44, 47, 67, 69, 18, 46, 19, 49, 68, 51,
        48, 70, 50, 71,
    ),
    (
        0, 1, 2, 3, 4, 5, 8, 9, 10, 11, 12, 13, 28, 29, 30, 31, 6, 7, 32, 33, 34, 35, 36, 37,
        38, 39, 60, 63, 61, 64, 26, 20, 62, 65, 58, 52, 14, 15, 21, 40, 41, 53, 16, 42, 43, 72, 17, 45,
        66, 18, 47, 44, 25, 19, 49, 57, 67, 24, 69, 22, 56, 46, 51, 54, 23, 74, 48, 70, 27, 55, 68, 59,
        71, 50, 73, 75,
    ),
    (
        0, 1, 2, 3, 4, 5, 8, 9, 10, 11, 12, 13, 28, 29, 30, 31, 6, 7, 32, 33, 34, 35, 36, 37,
        38, 39, 60, 63, 61, 64, 22, 62, 65, 25, 54, 14, 57, 23, 15, 40, 41, 16, 43, 55, 42, 73, 17, 45,
        66, 26, 18, 47, 58, 44, 19, 49, 67, 20, 69, 46, 21, 52, 51, 27, 24, 53, 48, 59, 70, 68, 50, 71,
        56, 72, 75, 74,
    ),
    (
        0, 1, 2, 3, 4, 5, 8, 6, 7, 22, 23, 20, 21, 9, 14, 54, 28, 29, 55, 10, 26, 40, 41, 52,
        53, 11, 30, 31, 27, 73, 58, 12, 33, 60, 15, 72, 59, 32, 35, 13, 75, 37, 66, 24, 34, 43, 16, 61,
        63, 25, 36, 39, 56, 42, 64, 57, 45, 62, 38, 65, 17, 74, 44, 18, 47, 67, 49, 46, 69, 19, 68, 70,
        48, 51, 50, 71,
    ),
    (
        0, 1, 2, 3, 4, 5, 8, 6, 7, 14, 28, 29, 9, 15, 40, 41, 31, 20, 60, 10, 43, 16, 52, 30,
        33, 45, 42, 21, 11, 17, 66, 35, 53, 12, 32, 24, 72, 47, 18, 44, 13, 56, 63, 25, 61, 37, 67, 19,
        57, 69, 26, 22, 34, 74, 49, 46, 58, 39, 36, 27, 23, 64, 54, 62, 51, 48, 70, 59, 68, 65, 55, 38,
        71, 75, 50, 73,
    ),
    (
        0, 1, 2, 3, 4, 5, 8, 6, 7, 9, 28, 29, 20, 30, 31, 10, 52, 60, 33, 21, 61, 11, 24, 53,
        35, 32, 12, 34, 63, 56, 72, 25, 13, 62, 37, 22, 36, 57, 39, 23, 54, 38, 64, 14, 74, 65, 40, 55,
        41, 66, 26, 73, 15, 58, 16, 17, 42, 43, 27, 18, 19, 44, 45, 59, 47, 46, 49, 67, 51, 75, 48, 69,
        50, 70, 68, 71,
    ),
    (
        0, 1, 2, 3, 4, 5, 8, 6, 7, 28, 29, 9, 14, 60, 31, 20, 30, 10, 41, 52, 40, 33, 21, 61,
        11, 35, 32, 53, 12, 66, 63, 24, 13, 72, 34, 37, 56, 15, 62, 39, 25, 36, 64, 16, 57, 38, 43, 26,
        22, 74, 42, 65, 17, 58, 44, 45, 27, 54, 67, 18, 23, 47, 19, 46, 59, 49, 55, 68, 69, 75, 73, 48,
        51, 70, 50, 71,
    ),
    (
        0, 1, 2, 3, 4, 5, 8, 6, 7, 14, 28, 29, 9, 41, 15, 40, 20, 31, 24, 60, 10, 43, 52, 16,
        30, 33, 56, 21, 42, 25, 45, 11, 17, 66, 53, 35, 32, 57, 18, 12, 47, 44, 72, 22, 63, 19, 23, 61,
        74, 54, 13, 49, 67, 69, 55, 34, 26, 37, 73, 46, 58, 27, 51, 62, 70, 48, 59, 39, 36, 75, 64, 68,
        71, 50, 65, 38,
    ),
    (
        0, 1, 2, 3, 4, 5, 8, 6, 7, 9, 28, 29, 10, 30, 31, 11, 33, 60, 12, 32, 35, 37, 61, 13,
        34, 63, 22, 14, 24, 36, 64, 54, 56, 39, 62, 23, 38, 41, 15, 27, 65, 55, 40, 43, 16, 59, 42, 73,
        45, 66, 26, 17, 58, 44, 18, 47, 20, 75, 67, 52, 19, 49, 46, 21, 69, 25, 53, 68, 51, 48, 57, 50,
        70, 72, 71, 74,
    ),
    (
        0, 1, 2, 3, 4, 5, 8, 9, 10, 11, 12, 13, 28, 29, 30, 31, 6, 7, 20, 22, 21, 23, 32, 33,
        52, 26, 54, 34, 35, 53, 27, 55, 36, 37, 14, 38, 39, 58, 72, 59, 15, 60, 63, 73, 75, 61, 64, 41,
        62, 24, 40, 65, 16, 25, 42, 43, 56, 45, 66, 57, 17, 44, 74, 47, 67, 18, 69, 46, 49, 68, 19, 70,
        48, 51, 50, 71,
    ),
)


def _steps():
    qs, ns, two = range(6), range(2), range(2)
    steps = [("ws", q) for q in qs] + [("ts", a) for a in two]
    steps += [("wo", n, q) for n in ns for q in qs]
    steps += [("tn", n, cc, a) for n in ns for cc in two for a in two]
    steps += [("wn", n, q, way) for n in ns for q in qs for way in two]
    steps += [("tx", n, cc, a) for n in ns for cc in two for a in two]
    steps += [("wl", n, q) for n in ns for q in qs] + [("tw", n, cc) for n in ns for cc in two]
    return steps


STEPS = _steps()


def mod(a, n):
    return lax.rem(a + 2 * n, n)


def coords():
    dp = lax.axis_index("dp")
    t = lax.axis_index("tensor")
    z_hi, y = dp // 4, lax.rem(dp, 4)
    z_lo, x, c = t // 8, lax.rem(t // 2, 4), lax.rem(t, 2)
    return x, y, 2 * z_hi + z_lo, c


def device(x, y, z, c):
    if isinstance(z, int):
        return ((z // 2) * 4 + y, (z % 2) * 8 + x * 2 + c)
    return ((z // 2) * 4 + y, lax.rem(z, 2) * 8 + x * 2 + c)


def carried(z, c):
    z_hi, z_lo = z // 2, z % 2
    s = (c + z_hi) % 2
    zs = ((z_hi + s) % 4, (z_hi + s + 2) % 4)
    return zs[::-1] if s and z_lo == 0 else zs


def gather_kernel(
    li, og, wg, wu, wd, po, pin, gain, lens,
    out,
    tok, bwg, bwu, bwd, bpo, acc_g, acc_u, acc_b, acc_l, acc_o, src_n, src_g, sq_mine, sq_all,
    r_tok, r_w, r_po, r_sq, s_all, s_po, s_sq,
):
    x, y, z, c = coords()
    z_hi, z_lo = z // 2, lax.rem(z, 2)
    xp, xm, yp, ym = mod(x + 1, 4), mod(x - 1, 4), mod(y + 1, 4), mod(y - 1, 4)
    other = (x, y, z, 1 - c)
    z1 = mod(z + 1 - 2 * z_lo, 8)
    ka, kc = lax.rem(z_hi, 2), z_hi // 2

    barrier = pltpu.get_barrier_semaphore()
    peers = [(x, yp, z, c), (x, ym, z, c), other]
    for dz in range(1, 8):
        for cc in (0, 1):
            peers.append((x, y, mod(z + dz, 8), cc))
    for dx in range(1, 4):
        for zz in (z, z1):
            for cc in (0, 1):
                peers.append((mod(x + dx, 4), y, zz, cc))
    for p in peers:
        pl.semaphore_signal(barrier, inc=1, device_id=device(*p), device_id_type=MESH)
    pl.semaphore_wait(barrier, len(peers))

    def remote(src, dst, ssem, rsem, to):
        return pltpu.make_async_remote_copy(
            src_ref=src, dst_ref=dst, send_sem=ssem, recv_sem=rsem,
            device_id=device(*to), device_id_type=MESH,
        )

    def arrived(ref, sem):
        pltpu.make_async_copy(ref, ref, sem).wait()

    chunks = [(0, 0), (1, 0), (2, 0), (0, 1), (1, 1), (2, 1)]

    def wslot(j, q):
        m, h = chunks[q]
        n = KB // 2 if m < 2 else HID // 2
        return (bwg, bwu, bwd)[m].at[j, pl.ds(h * n, n)]

    def wsrc(q):
        m, h = chunks[q]
        n = KB // 2 if m < 2 else HID // 2
        return (wg, wu, wd)[m].at[pl.ds(h * n, n)]

    def walk(z, c, numbers, first, drain):
        z_hi, z_lo = z // 2, z % 2
        ka, z1 = z_hi % 2, z ^ 1
        zs = carried(z, c)
        kt = z_lo + 2 * c
        rel, f = (z_hi - kt) % 4, z_hi % 2
        entry = 1 if rel == 1 else 0 if rel == 3 else 1 - z_lo
        far = z1 if rel == 0 else 2 * kt + entry
        b, i = z_hi % 2, z_hi // 2
        hop = 2 if z_lo == b else 1
        r0 = (z - 2 * z_lo - 4 * c) % 8
        u0 = 1 - ((r0 + 7) % 8) // 4
        us = (u0, 1 - u0)
        count = [first]

        def send(src, dst, rsem, to):
            d = remote(src, dst, s_all.at[count[0]], rsem, to)
            count[0] += 1
            d.wait_send() if drain else d.start()

        def await_(ref, sem):
            if not drain:
                arrived(ref, sem)

        for number in numbers:
            kind, *arg = STEPS[number]
            if kind == "ws":
                j, q = z_hi * 4 + y, arg[0]
                if rel == 0 and f != c:
                    send(wsrc(q), wslot(j, q), r_w.at[j, q], (x, y, z, 1 - c))
                if rel == 0 and f == c and not drain:
                    pltpu.make_async_copy(wsrc(q), wslot(j, q), r_w.at[j, q]).start()
                send(wsrc(q), wslot(j, q), r_w.at[j, q], (x, y, far, f))
            elif kind == "ts":
                a = arg[0]
                j = z_lo * 8 + x * 2 + c
                src, dst, sem = (src_n, src_g)[a], tok.at[a, j], r_tok.at[a, j]
                if hop == 2 and i != c:
                    send(src, dst, sem, (x, y, z, i))
                if hop == 2 and i == c and not drain:
                    pltpu.make_async_copy(src, dst, sem).start()
                send(src, dst, sem, (x, y, (z + hop) % 8, i))
                send(src, dst, sem, (x, y, (z - hop) % 8, i))
            elif kind == "wo":
                n, q = arg
                j, r = zs[n] * 4 + y, (zs[n] - z_hi) % 4
                ent = 1 if r == 1 else 0 if r == 3 else 1 - ka
                blk, sem = wslot(j, q), r_w.at[j, q]
                await_(blk, sem)
                if r != 0 and z_lo == ent:
                    send(blk, blk, sem, (x, y, z1, c))
                send(blk, blk, sem, (x, yp, z, c))
                send(blk, blk, sem, (x, ym, z, c))
                send(blk, blk, sem, (x, y, z, 1 - c))
            elif kind == "wn":
                n, q, way = arg
                j = zs[n] * 4 + (ym, yp)[way]
                blk, sem = wslot(j, q), r_w.at[j, q]
                await_(blk, sem)
                if q // 3 == way:
                    send(blk, blk, sem, (x, (yp, ym)[way], z, c))
                send(blk, blk, sem, (x, y, z, 1 - c))
            elif kind == "wl":
                n, q = arg
                j = zs[n] * 4 + mod(y + 2, 4)
                blk, sem = wslot(j, q), r_w.at[j, q]
                await_(blk, sem)
                send(blk, blk, sem, (x, y, z, 1 - c))
            elif kind == "tn":
                n, cc, a = arg
                u = us[n]
                r = (r0 - u) % 8
                j = u * 8 + x * 2 + cc
                blk, sem = tok.at[a, j], r_tok.at[a, j]
                await_(blk, sem)
                if r in ((1, 2), (1,))[a]:
                    send(blk, blk, sem, (x, y, (z + 2) % 8, c))
                if r in ((7,), (6, 7))[a]:
                    send(blk, blk, sem, (x, y, (z - 2) % 8, c))
                send(blk, blk, sem, (xp, y, z, c))
                send(blk, blk, sem, (xm, y, z, c))
            elif kind == "tx":
                n, cc, a = arg
                j = us[n] * 8 + (xm, xp)[a] * 2 + cc
                blk, sem = tok.at[a, j], r_tok.at[a, j]
                await_(blk, sem)
                send(blk, blk, sem, ((xp, xm)[a], y, z, c))
            elif kind == "tw":
                n, cc = arg
                for a in (0, 1):
                    for xx in ((xp, xm)[a], mod(x + 2, 4)):
                        j = us[n] * 8 + xx * 2 + cc
                        await_(tok.at[a, j], r_tok.at[a, j])
        return count[0]

    sent = {}

    def everyone(part, drain=False):
        for zz in range(8):
            for cc in range(2):
                order = ORDERS[zz * 2 + cc]
                cut = min(order.index(n) for n, s in enumerate(STEPS) if s[0] == "ts")
                numbers = (order[:cut], order[cut:])[part]
                first = sent[zz, cc] if part else 0

                def go(zz=zz, cc=cc, numbers=numbers, first=first):
                    sent[zz, cc] = walk(zz, cc, numbers, first, drain)

                pl.when((z == zz) & (c == cc))(go)

    v = li[...].astype(F32)
    ones = jnp.ones((8, KB), F32)
    row = lax.dot_general(
        ones, v * v, (((1,), (1,)), ((), ())), precision=lax.Precision.HIGHEST, preferred_element_type=F32
    )
    sq_mine[...] = row[0:1, :]
    t_me = z_lo * 8 + x * 2 + c
    sq_sends = []
    for d in range(1, 16):
        to = (mod(x + (d // 2) % 4, 4), y, (z, z1)[d // 8], lax.rem(c + d % 2, 2))
        sq_sends.append(remote(sq_mine, sq_all.at[t_me], s_sq.at[d], r_sq.at[t_me], to))
        sq_sends[-1].start()
    everyone(0)

    has_po = (z_lo == ka) & (c == kc)
    po_sends = [
        remote(po, bpo, s_po.at[0], r_po, other),
        remote(po, bpo, s_po.at[1], r_po, (x, y, z1, 0)),
        remote(po, bpo, s_po.at[2], r_po, (x, y, z1, 1)),
    ]

    def start_po():
        for d in po_sends:
            d.start()
        pltpu.make_async_copy(po, bpo, r_po).start()

    pl.when(has_po)(start_po)

    at = lax.broadcasted_iota(jnp.int32, (TOK, KB), 0)
    count = jnp.where(at < TOK // 2, lens[0, 0], lens[0, 1])
    valid = (at % (TOK // 2)) < count
    src_g[...] = jnp.where(valid, og[...].astype(F32), 0.0).astype(BF16)
    total = row[0:1, :]
    for d in range(1, 16):
        t = lax.rem(z_lo + d // 8, 2) * 8 + mod(x + (d // 2) % 4, 4) * 2 + lax.rem(c + d % 2, 2)
        arrived(sq_all.at[t], r_sq.at[t])
        total = total + sq_all[t]
    factor = lax.rsqrt(total * (1.0 / 4096.0) + 1e-05)
    factor = jnp.transpose(jnp.broadcast_to(factor, (8, TOK)), (1, 0))[:, 0:1]
    src_n[...] = (v * factor * gain[t_me]).astype(BF16)

    everyone(1)
    arrived(bpo, r_po)

    for ref in (acc_g, acc_u, acc_b, acc_l, acc_o):
        ref[...] = jnp.zeros_like(ref)
    carry = lax.rem(c + z_hi, 2)

    @pl.loop(0, NB)
    def _(s):
        rest = s // 8
        zz = mod(z_hi + carry + rest + 2 * (lax.rem(s, 8) // 4), 4)
        j = zz * 4 + mod(y + lax.rem(s, 4), 4)

        def wait_rest():
            for q in range(6):
                arrived(wslot(j, q), r_w.at[j, q])

        pl.when(rest == 1)(wait_rest)
        n = tok[0, j]
        acc_g[...] += jnp.dot(n, bwg[j], preferred_element_type=F32)
        acc_u[...] += jnp.dot(n, bwu[j], preferred_element_type=F32)
        acc_l[...] += jnp.dot(n, pin[j], preferred_element_type=F32)
        acc_b[...] += lax.dot_general(
            tok[1, j], bwd[j], (((1,), (1,)), ((), ())), preferred_element_type=F32
        )

    @pl.loop(0, TOK // 128)
    def _(t):
        rows = pl.ds(pl.multiple_of(t * 128, 128), 128)
        gate = acc_g[rows, :]
        sig = 1.0 / (1.0 + jnp.exp(-gate))
        dgate = (acc_b[rows, :] * acc_u[rows, :] * sig * (1.0 + gate * (1.0 - sig))).astype(BF16)
        right = lax.dot_general(
            dgate, bpo[...], (((1,), (1,)), ((), ())), preferred_element_type=F32
        )
        acc_o[...] += lax.dot_general(
            acc_l[rows, :], right, (((0,), (0,)), ((), ())),
            precision=lax.Precision.HIGHEST, preferred_element_type=F32,
        )

    for j in range(NB):
        out[j] = acc_o[4 * j:4 * j + 4, :]

    everyone(0, drain=True)
    everyone(1, drain=True)
    for d in sq_sends:
        d.wait_send()

    def wait_po():
        for d in po_sends:
            d.wait_send()

    pl.when(has_po)(wait_po)


def finish_kernel(part, q, grad, score, got1, mine, got2, got3, got4, rows, r1, r2, r3, r4, s1, s2, s3, s4):
    x, y, z, c = coords()
    z_hi, z_lo = z // 2, lax.rem(z, 2)
    ph = z_lo + 2 * c
    piece = z_hi * 4 + x

    def dev2(zh, yy, zl, xx, cc):
        return (zh * 4 + yy, zl * 8 + xx * 2 + cc)

    team = [(mod(z_hi + d // 4, 4), mod(x + d % 4, 4)) for d in range(1, 16)]
    same_t = [(mod(z_hi + d // 4, 4), mod(y + d % 4, 4)) for d in range(1, 16)]
    every_t = [(lax.rem(z_lo + d // 8, 2), mod(x + (d // 2) % 4, 4), lax.rem(c + d % 2, 2)) for d in range(16)]
    barrier = pltpu.get_barrier_semaphore()

    def tell(to):
        pl.semaphore_signal(barrier, inc=1, device_id=to, device_id_type=MESH)

    for zh, xx in team:
        tell(dev2(zh, y, z_lo, xx, c))
    for zh, yy in same_t:
        tell(dev2(zh, yy, z_lo, x, c))
    for d in range(16):
        tell(dev2(d // 4, y, lax.rem(z_hi, 2), d % 4, z_hi // 2))
        tell(dev2(z_hi, d // 4, d % 2, y, (d // 2) % 2))
    pl.semaphore_wait(barrier, 62)
    waits = []

    def send(src, dst, ssem, rsem, to, self_=None):
        d = pltpu.make_async_remote_copy(
            src_ref=src, dst_ref=dst, send_sem=ssem, recv_sem=rsem, device_id=to, device_id_type=MESH,
        )
        if self_ is None:
            d.start()
            waits.append(d.wait_send)
        else:
            def stay():
                pltpu.make_async_copy(src, dst, rsem).start()

            pl.when(jnp.logical_not(self_))(lambda: d.start())
            pl.when(self_)(stay)
            waits.append(lambda: pl.when(jnp.logical_not(self_))(lambda: d.wait_send()))

    def arrived(ref, sem):
        pltpu.make_async_copy(ref, ref, sem).wait()

    for n, (zh, xx) in enumerate(team):
        send(part.at[zh * 4 + xx], got1.at[piece], s1.at[n], r1.at[piece], dev2(zh, y, z_lo, xx, c))
    total = part[piece]
    for zh, xx in team:
        m = zh * 4 + xx
        arrived(got1.at[m], r1.at[m])
        total = total + got1[m]
    mine[...] = total
    pair = ph * 4 + y
    for n, (zl, xx, cc) in enumerate(every_t):
        send(mine, got3.at[pair], s3.at[n], r3.at[pair], dev2(z_hi, x, zl, xx, cc), (x == y) if n == 0 else None)
    for n, (zl, xx, cc) in enumerate(every_t):
        send(mine, got2.at[piece], s2.at[n], r2.at[piece], dev2(ph, y, zl, xx, cc), (ph == z_hi) if n == 0 else None)
    for p in range(16):
        arrived(got3.at[p], r3.at[p])
    s = jnp.zeros((16, KB), F32)
    for r in range(4):
        f = got3[:, r, :].astype(BF16)
        s = s + lax.dot_general(
            f, q[:, r * RANK:(r + 1) * RANK], (((1,), (1,)), ((), ())), preferred_element_type=F32
        )
    for p in range(16):
        rows[p] = s[p:p + 1, :]
    me = z_hi * 4 + y
    for n, (zh, yy) in enumerate(same_t):
        send(rows.at[zh * 4 + yy], got4.at[me], s4.at[n], r4.at[me], dev2(zh, yy, z_lo, x, c))
    for p in range(16):
        arrived(got2.at[p], r2.at[p])
        grad[p] = got2[p]
    total = rows[me]
    for zh, yy in same_t:
        m = zh * 4 + yy
        arrived(got4.at[m], r4.at[m])
        total = total + got4[m]
    score[...] = total
    for w in waits:
        w()


def finish(part, queries):
    vmem = pl.BlockSpec(memory_space=pltpu.VMEM)
    dma = pltpu.SemaphoreType.DMA
    piece = pltpu.VMEM((NB, 4, RANK), F32)
    row = pltpu.VMEM((16, 1, KB), F32)
    return pl.pallas_call(
        finish_kernel,
        out_shape=(
            jax.ShapeDtypeStruct((NB, 4, RANK), F32),
            jax.ShapeDtypeStruct((1, KB), F32),
        ),
        in_specs=[vmem] * 2,
        out_specs=(vmem, vmem),
        scratch_shapes=[piece, pltpu.VMEM((4, RANK), F32), piece, piece, row, row]
        + [dma((16,))] * 8,
        compiler_params=pltpu.CompilerParams(collective_id=1, has_side_effects=True),
    )(part, queries)


def gathered(li, og, wg, wu, wd, po, pin, gain, lens):
    any_ = pl.BlockSpec(memory_space=pl.ANY)
    vmem = pl.BlockSpec(memory_space=pltpu.VMEM)
    smem = pl.BlockSpec(memory_space=pltpu.SMEM)
    dma = pltpu.SemaphoreType.DMA
    return pl.pallas_call(
        gather_kernel,
        out_shape=jax.ShapeDtypeStruct((NB, 4, RANK), F32),
        in_specs=[vmem] * 2 + [any_] * 4 + [vmem] * 2 + [smem],
        out_specs=vmem,
        scratch_shapes=[
            pltpu.VMEM((2, NB, TOK, KB), BF16),
            pltpu.VMEM((NB, KB, HID), BF16),
            pltpu.VMEM((NB, KB, HID), BF16),
            pltpu.VMEM((NB, HID, KB), BF16),
            pltpu.VMEM((RANK, HID), BF16),
            pltpu.VMEM((TOK, HID), F32),
            pltpu.VMEM((TOK, HID), F32),
            pltpu.VMEM((TOK, HID), F32),
            pltpu.VMEM((TOK, RANK), F32),
            pltpu.VMEM((RANK, RANK), F32),
            pltpu.VMEM((TOK, KB), BF16),
            pltpu.VMEM((TOK, KB), BF16),
            pltpu.VMEM((1, TOK), F32),
            pltpu.VMEM((16, 1, TOK), F32),
            dma((2, NB)),
            dma((NB, 6)),
            dma,
            dma((16,)),
            dma((NSEND,)),
            dma((3,)),
            dma((16,)),
        ],
        compiler_params=pltpu.CompilerParams(
            collective_id=0, has_side_effects=True, vmem_limit_bytes=60 << 20
        ),
    )(li, og, wg, wu, wd, po, pin, gain, lens)


def on_device(
    layer_input,
    out_grad,
    norm_gain,
    gate_weight,
    up_weight,
    down_weight,
    lengths,
    proj_in,
    proj_out,
    queries,
):
    part = gathered(
        layer_input.reshape(TOK, KB),
        out_grad.reshape(TOK, KB),
        gate_weight,
        up_weight,
        down_weight,
        proj_out.T,
        proj_in.reshape(NB, KB, RANK),
        norm_gain.reshape(NB, 1, KB),
        lengths,
    )
    grad, scores = finish(part, queries)
    return (grad.reshape(1, RANK, RANK), scores)


def solution(mesh):
    in_specs = (
        P("dp", None, None, "tensor"),
        P("dp", None, None, "tensor"),
        P(),
        P("dp", "tensor"),
        P("dp", "tensor"),
        P("tensor", "dp"),
        P("dp", None),
        P(),
        P("tensor", None),
        P("tensor", "dp"),
    )
    out_specs = (P("dp", None, None), P("dp", "tensor"))
    return jax.shard_map(
        on_device, mesh=mesh, in_specs=in_specs, out_specs=out_specs, check_vma=False
    )
```

```python
import jax
import jax.numpy as jnp
from jax import lax
from jax.experimental import pallas as pl
from jax.experimental.pallas import tpu as pltpu
from jax.sharding import PartitionSpec as P

MESH = pl.DeviceIdType.MESH
F32 = jnp.float32
BF16 = jnp.bfloat16
TOK = 512
KB = 256
NB = 16
HID = 896
RANK = 64
NSEND = 176

ORDERS = (
    (
        0, 1, 2, 3, 4, 5, 8, 9, 10, 11, 12, 13, 28, 29, 30, 31, 6, 7, 22, 20, 23, 21, 32, 33,
        54, 24, 52, 34, 35, 55, 25, 53, 36, 37, 14, 38, 39, 56, 73, 57, 15, 60, 63, 72, 74, 61, 64, 41,
        62, 16, 26, 40, 65, 42, 43, 27, 58, 44, 45, 59, 17, 66, 75, 18, 47, 67, 49, 68, 69, 46, 19, 70,
        48, 51, 50, 71,
    ),
    (
        0, 1, 2, 3, 4, 5, 8, 6, 7, 9, 28, 29, 10, 30, 31, 11, 33, 60, 12, 32, 35, 37, 61, 13,
        34, 63, 14, 20, 27, 36, 64, 52, 24, 59, 39, 62, 38, 41, 21, 15, 65, 56, 40, 43, 16, 53, 42, 72,
        17, 45, 66, 47, 44, 18, 22, 25, 67, 69, 54, 19, 57, 23, 46, 49, 74, 26, 68, 51, 55, 48, 58, 70,
        50, 73, 75, 71,
    ),
    (
        0, 1, 2, 3, 4, 5, 8, 6, 7, 14, 28, 29, 9, 41, 15, 40, 22, 31, 26, 60, 10, 43, 54, 16,
        30, 33, 58, 23, 42, 27, 45, 11, 17, 66, 55, 35, 32, 59, 18, 12, 47, 44, 73, 20, 63, 19, 21, 61,
        75, 52, 13, 49, 67, 37, 53, 34, 24, 69, 72, 46, 56, 25, 51, 62, 39, 48, 57, 70, 36, 74, 64, 68,
        71, 50, 65, 38,
    ),
    (
        0, 1, 2, 3, 4, 5, 8, 6, 7, 28, 29, 9, 14, 60, 31, 22, 30, 10, 41, 54, 40, 33, 23, 11,
        61, 35, 32, 55, 12, 63, 66, 26, 13, 73, 37, 34, 58, 15, 39, 62, 27, 64, 36, 16, 59, 43, 38, 24,
        65, 20, 75, 42, 17, 45, 56, 44, 47, 25, 52, 67, 18, 21, 19, 69, 46, 57, 53, 49, 68, 74, 72, 51,
        48, 70, 50, 71,
    ),
    (
        0, 1, 2, 3, 4, 5, 8, 6, 7, 9, 28, 29, 22, 30, 31, 10, 54, 60, 33, 23, 61, 11, 26, 55,
        35, 32, 34, 63, 58, 12, 73, 27, 13, 62, 37, 20, 36, 59, 39, 21, 52, 38, 64, 14, 75, 65, 40, 53,
        41, 66, 24, 72, 15, 16, 56, 17, 42, 43, 25, 18, 19, 44, 45, 57, 47, 46, 49, 67, 51, 74, 48, 69,
        50, 70, 68, 71,
    ),
    (
        0, 1, 2, 3, 4, 5, 8, 6, 7, 14, 28, 29, 9, 15, 40, 41, 31, 22, 60, 10, 43, 16, 54, 30,
        33, 45, 42, 23, 11, 17, 66, 35, 55, 12, 26, 32, 47, 73, 18, 44, 13, 63, 58, 27, 61, 37, 67, 19,
        59, 69, 24, 20, 34, 49, 75, 46, 56, 39, 25, 21, 36, 52, 64, 62, 51, 48, 70, 57, 68, 53, 65, 38,
        74, 71, 50, 72,
    ),
    (
        0, 1, 2, 3, 4, 5, 8, 6, 7, 20, 21, 22, 23, 9, 14, 52, 28, 29, 53, 10, 24, 40, 41, 54,
        55, 11, 30, 31, 25, 72, 56, 12, 33, 60, 15, 73, 57, 32, 35, 13, 74, 37, 66, 26, 34, 43, 16, 61,
        63, 27, 58, 36, 39, 42, 64, 59, 45, 62, 17, 75, 38, 65, 44, 47, 67, 69, 18, 46, 19, 49, 68, 51,
        48, 70, 50, 71,
    ),
    (
        0, 1, 2, 3, 4, 5, 8, 9, 10, 11, 12, 13, 28, 29, 30, 31, 6, 7, 32, 33, 34, 35, 36, 37,
        38, 39, 60, 63, 61, 64, 26, 20, 62, 65, 58, 52, 14, 15, 21, 40, 41, 53, 16, 42, 43, 72, 17, 45,
        66, 18, 47, 44, 25, 19, 49, 57, 67, 24, 69, 22, 56, 46, 51, 54, 23, 74, 48, 70, 27, 55, 68, 59,
        71, 50, 73, 75,
    ),
    (
        0, 1, 2, 3, 4, 5, 8, 9, 10, 11, 12, 13, 28, 29, 30, 31, 6, 7, 32, 33, 34, 35, 36, 37,
        38, 39, 60, 63, 61, 64, 22, 62, 65, 25, 54, 14, 57, 23, 15, 40, 41, 16, 43, 55, 42, 73, 17, 45,
        66, 26, 18, 47, 58, 44, 19, 49, 67, 20, 69, 46, 21, 52, 51, 27, 24, 53, 48, 59, 70, 68, 50, 71,
        56, 72, 75, 74,
    ),
    (
        0, 1, 2, 3, 4, 5, 8, 6, 7, 22, 23, 20, 21, 9, 14, 54, 28, 29, 55, 10, 26, 40, 41, 52,
        53, 11, 30, 31, 27, 73, 58, 12, 33, 60, 15, 72, 59, 32, 35, 13, 75, 37, 66, 24, 34, 43, 16, 61,
        63, 25, 36, 39, 56, 42, 64, 57, 45, 62, 38, 65, 17, 74, 44, 18, 47, 67, 49, 46, 69, 19, 68, 70,
        48, 51, 50, 71,
    ),
    (
        0, 1, 2, 3, 4, 5, 8, 6, 7, 14, 28, 29, 9, 15, 40, 41, 31, 20, 60, 10, 43, 16, 52, 30,
        33, 45, 42, 21, 11, 17, 66, 35, 53, 12, 32, 24, 72, 47, 18, 44, 13, 56, 63, 25, 61, 37, 67, 19,
        57, 69, 26, 22, 34, 74, 49, 46, 58, 39, 36, 27, 23, 64, 54, 62, 51, 48, 70, 59, 68, 65, 55, 38,
        71, 75, 50, 73,
    ),
    (
        0, 1, 2, 3, 4, 5, 8, 6, 7, 9, 28, 29, 20, 30, 31, 10, 52, 60, 33, 21, 61, 11, 24, 53,
        35, 32, 12, 34, 63, 56, 72, 25, 13, 62, 37, 22, 36, 57, 39, 23, 54, 38, 64, 14, 74, 65, 40, 55,
        41, 66, 26, 73, 15, 58, 16, 17, 42, 43, 27, 18, 19, 44, 45, 59, 47, 46, 49, 67, 51, 75, 48, 69,
        50, 70, 68, 71,
    ),
    (
        0, 1, 2, 3, 4, 5, 8, 6, 7, 28, 29, 9, 14, 60, 31, 20, 30, 10, 41, 52, 40, 33, 21, 61,
        11, 35, 32, 53, 12, 66, 63, 24, 13, 72, 34, 37, 56, 15, 62, 39, 25, 36, 64, 16, 57, 38, 43, 26,
        22, 74, 42, 65, 17, 58, 44, 45, 27, 54, 67, 18, 23, 47, 19, 46, 59, 49, 55, 68, 69, 75, 73, 48,
        51, 70, 50, 71,
    ),
    (
        0, 1, 2, 3, 4, 5, 8, 6, 7, 14, 28, 29, 9, 41, 15, 40, 20, 31, 24, 60, 10, 43, 52, 16,
        30, 33, 56, 21, 42, 25, 45, 11, 17, 66, 53, 35, 32, 57, 18, 12, 47, 44, 72, 22, 63, 19, 23, 61,
        74, 54, 13, 49, 67, 69, 55, 34, 26, 37, 73, 46, 58, 27, 51, 62, 70, 48, 59, 39, 36, 75, 64, 68,
        71, 50, 65, 38,
    ),
    (
        0, 1, 2, 3, 4, 5, 8, 6, 7, 9, 28, 29, 10, 30, 31, 11, 33, 60, 12, 32, 35, 37, 61, 13,
        34, 63, 22, 14, 24, 36, 64, 54, 56, 39, 62, 23, 38, 41, 15, 27, 65, 55, 40, 43, 16, 59, 42, 73,
        45, 66, 26, 17, 58, 44, 18, 47, 20, 75, 67, 52, 19, 49, 46, 21, 69, 25, 53, 68, 51, 48, 57, 50,
        70, 72, 71, 74,
    ),
    (
        0, 1, 2, 3, 4, 5, 8, 9, 10, 11, 12, 13, 28, 29, 30, 31, 6, 7, 20, 22, 21, 23, 32, 33,
        52, 26, 54, 34, 35, 53, 27, 55, 36, 37, 14, 38, 39, 58, 72, 59, 15, 60, 63, 73, 75, 61, 64, 41,
        62, 24, 40, 65, 16, 25, 42, 43, 56, 45, 66, 57, 17, 44, 74, 47, 67, 18, 69, 46, 49, 68, 19, 70,
        48, 51, 50, 71,
    ),
)


def _steps():
    qs, ns, two = range(6), range(2), range(2)
    steps = [("ws", q) for q in qs] + [("ts", a) for a in two]
    steps += [("wo", n, q) for n in ns for q in qs]
    steps += [("tn", n, cc, a) for n in ns for cc in two for a in two]
    steps += [("wn", n, q, way) for n in ns for q in qs for way in two]
    steps += [("tx", n, cc, a) for n in ns for cc in two for a in two]
    steps += [("wl", n, q) for n in ns for q in qs] + [("tw", n, cc) for n in ns for cc in two]
    return steps


STEPS = _steps()


def mod(a, n):
    return lax.rem(a + 2 * n, n)


def coords():
    dp = lax.axis_index("dp")
    t = lax.axis_index("tensor")
    z_hi, y = dp // 4, lax.rem(dp, 4)
    z_lo, x, c = t // 8, lax.rem(t // 2, 4), lax.rem(t, 2)
    return x, y, 2 * z_hi + z_lo, c


def device(x, y, z, c):
    if isinstance(z, int):
        return ((z // 2) * 4 + y, (z % 2) * 8 + x * 2 + c)
    return ((z // 2) * 4 + y, lax.rem(z, 2) * 8 + x * 2 + c)


def at5(zh, yy, zl, xx, cc):
    return (zh * 4 + yy, zl * 8 + xx * 2 + cc)


def carried(z, c):
    z_hi, z_lo = z // 2, z % 2
    s = (c + z_hi) % 2
    zs = ((z_hi + s) % 4, (z_hi + s + 2) % 4)
    return zs[::-1] if s and z_lo == 0 else zs


def gather_kernel(
    li, og, wg, wu, wd, po, pin, gain, lens, q,
    grad, score,
    tok, bwg, bwu, bwd, bpo, acc_g, acc_u, acc_b, acc_l, acc_o, src_n, src_g, sq_mine, sq_all,
    part, got1, mine, got2, got3, got4, rows4,
    r_tok, r_w, r_po, r_sq, s_all, s_po, s_sq, r1, r2, r3, r4, s1, s2, s3, s4,
):
    x, y, z, c = coords()
    z_hi, z_lo = z // 2, lax.rem(z, 2)
    xp, xm, yp, ym = mod(x + 1, 4), mod(x - 1, 4), mod(y + 1, 4), mod(y - 1, 4)
    other = (x, y, z, 1 - c)
    z1 = mod(z + 1 - 2 * z_lo, 8)
    ka, kc = lax.rem(z_hi, 2), z_hi // 2

    barrier = pltpu.get_barrier_semaphore()
    peers = [(x, yp, z, c), (x, ym, z, c), other]
    for dz in range(1, 8):
        for cc in (0, 1):
            peers.append((x, y, mod(z + dz, 8), cc))
    for dx in range(1, 4):
        for zz in (z, z1):
            for cc in (0, 1):
                peers.append((mod(x + dx, 4), y, zz, cc))
    team = [(mod(z_hi + d // 4, 4), mod(x + d % 4, 4)) for d in range(1, 16)]
    same_t = [(mod(z_hi + d // 4, 4), mod(y + d % 4, 4)) for d in range(1, 16)]
    ends = [(zh, y, z_lo, xx, c) for zh, xx in team] + [(zh, yy, z_lo, x, c) for zh, yy in same_t]
    for d in range(16):
        ends.append((d // 4, y, lax.rem(z_hi, 2), d % 4, z_hi // 2))
        ends.append((z_hi, d // 4, d % 2, y, (d // 2) % 2))
    signals = [device(*p) for p in peers] + [at5(*p) for p in ends]
    for p in signals:
        pl.semaphore_signal(barrier, inc=1, device_id=p, device_id_type=MESH)
    pl.semaphore_wait(barrier, len(signals))

    def remote(src, dst, ssem, rsem, to):
        return pltpu.make_async_remote_copy(
            src_ref=src, dst_ref=dst, send_sem=ssem, recv_sem=rsem,
            device_id=device(*to), device_id_type=MESH,
        )

    def arrived(ref, sem):
        pltpu.make_async_copy(ref, ref, sem).wait()

    chunks = [(0, 0), (1, 0), (2, 0), (0, 1), (1, 1), (2, 1)]

    def wslot(j, q):
        m, h = chunks[q]
        n = KB // 2 if m < 2 else HID // 2
        return (bwg, bwu, bwd)[m].at[j, pl.ds(h * n, n)]

    def wsrc(q):
        m, h = chunks[q]
        n = KB // 2 if m < 2 else HID // 2
        return (wg, wu, wd)[m].at[pl.ds(h * n, n)]

    def walk(z, c, numbers, first, drain):
        z_hi, z_lo = z // 2, z % 2
        ka, z1 = z_hi % 2, z ^ 1
        zs = carried(z, c)
        kt = z_lo + 2 * c
        rel, f = (z_hi - kt) % 4, z_hi % 2
        entry = 1 if rel == 1 else 0 if rel == 3 else 1 - z_lo
        far = z1 if rel == 0 else 2 * kt + entry
        b, i = z_hi % 2, z_hi // 2
        hop = 2 if z_lo == b else 1
        r0 = (z - 2 * z_lo - 4 * c) % 8
        u0 = 1 - ((r0 + 7) % 8) // 4
        us = (u0, 1 - u0)
        count = [first]

        def send(src, dst, rsem, to):
            d = remote(src, dst, s_all.at[count[0]], rsem, to)
            count[0] += 1
            d.wait_send() if drain else d.start()

        def await_(ref, sem):
            if not drain:
                arrived(ref, sem)

        for number in numbers:
            kind, *arg = STEPS[number]
            if kind == "ws":
                j, q = z_hi * 4 + y, arg[0]
                if rel == 0 and f != c:
                    send(wsrc(q), wslot(j, q), r_w.at[j, q], (x, y, z, 1 - c))
                if rel == 0 and f == c and not drain:
                    pltpu.make_async_copy(wsrc(q), wslot(j, q), r_w.at[j, q]).start()
                send(wsrc(q), wslot(j, q), r_w.at[j, q], (x, y, far, f))
            elif kind == "ts":
                a = arg[0]
                j = z_lo * 8 + x * 2 + c
                src, dst, sem = (src_n, src_g)[a], tok.at[a, j], r_tok.at[a, j]
                if hop == 2 and i != c:
                    send(src, dst, sem, (x, y, z, i))
                if hop == 2 and i == c and not drain:
                    pltpu.make_async_copy(src, dst, sem).start()
                send(src, dst, sem, (x, y, (z + hop) % 8, i))
                send(src, dst, sem, (x, y, (z - hop) % 8, i))
            elif kind == "wo":
                n, q = arg
                j, r = zs[n] * 4 + y, (zs[n] - z_hi) % 4
                ent = 1 if r == 1 else 0 if r == 3 else 1 - ka
                blk, sem = wslot(j, q), r_w.at[j, q]
                await_(blk, sem)
                if r != 0 and z_lo == ent:
                    send(blk, blk, sem, (x, y, z1, c))
                send(blk, blk, sem, (x, yp, z, c))
                send(blk, blk, sem, (x, ym, z, c))
                send(blk, blk, sem, (x, y, z, 1 - c))
            elif kind == "wn":
                n, q, way = arg
                j = zs[n] * 4 + (ym, yp)[way]
                blk, sem = wslot(j, q), r_w.at[j, q]
                await_(blk, sem)
                if q // 3 == way:
                    send(blk, blk, sem, (x, (yp, ym)[way], z, c))
                send(blk, blk, sem, (x, y, z, 1 - c))
            elif kind == "wl":
                n, q = arg
                j = zs[n] * 4 + mod(y + 2, 4)
                blk, sem = wslot(j, q), r_w.at[j, q]
                await_(blk, sem)
                send(blk, blk, sem, (x, y, z, 1 - c))
            elif kind == "tn":
                n, cc, a = arg
                u = us[n]
                r = (r0 - u) % 8
                j = u * 8 + x * 2 + cc
                blk, sem = tok.at[a, j], r_tok.at[a, j]
                await_(blk, sem)
                if r in ((1, 2), (1,))[a]:
                    send(blk, blk, sem, (x, y, (z + 2) % 8, c))
                if r in ((7,), (6, 7))[a]:
                    send(blk, blk, sem, (x, y, (z - 2) % 8, c))
                send(blk, blk, sem, (xp, y, z, c))
                send(blk, blk, sem, (xm, y, z, c))
            elif kind == "tx":
                n, cc, a = arg
                j = us[n] * 8 + (xm, xp)[a] * 2 + cc
                blk, sem = tok.at[a, j], r_tok.at[a, j]
                await_(blk, sem)
                send(blk, blk, sem, ((xp, xm)[a], y, z, c))
            elif kind == "tw":
                n, cc = arg
                for a in (0, 1):
                    for xx in ((xp, xm)[a], mod(x + 2, 4)):
                        j = us[n] * 8 + xx * 2 + cc
                        await_(tok.at[a, j], r_tok.at[a, j])
        return count[0]

    sent = {}

    def everyone(part, drain=False):
        for zz in range(8):
            for cc in range(2):
                order = ORDERS[zz * 2 + cc]
                cut = min(order.index(n) for n, s in enumerate(STEPS) if s[0] == "ts")
                numbers = (order[:cut], order[cut:])[part]
                first = sent[zz, cc] if part else 0

                def go(zz=zz, cc=cc, numbers=numbers, first=first):
                    sent[zz, cc] = walk(zz, cc, numbers, first, drain)

                pl.when((z == zz) & (c == cc))(go)

    v = li[...].astype(F32)
    ones = jnp.ones((8, KB), F32)
    row = lax.dot_general(
        ones, v * v, (((1,), (1,)), ((), ())), precision=lax.Precision.HIGHEST, preferred_element_type=F32
    )
    sq_mine[...] = row[0:1, :]
    t_me = z_lo * 8 + x * 2 + c
    sq_sends = []
    for d in range(1, 16):
        to = (mod(x + (d // 2) % 4, 4), y, (z, z1)[d // 8], lax.rem(c + d % 2, 2))
        sq_sends.append(remote(sq_mine, sq_all.at[t_me], s_sq.at[d], r_sq.at[t_me], to))
        sq_sends[-1].start()
    everyone(0)

    has_po = (z_lo == ka) & (c == kc)
    po_sends = [
        remote(po, bpo, s_po.at[0], r_po, other),
        remote(po, bpo, s_po.at[1], r_po, (x, y, z1, 0)),
        remote(po, bpo, s_po.at[2], r_po, (x, y, z1, 1)),
    ]

    def start_po():
        for d in po_sends:
            d.start()
        pltpu.make_async_copy(po, bpo, r_po).start()

    pl.when(has_po)(start_po)

    at = lax.broadcasted_iota(jnp.int32, (TOK, KB), 0)
    count = jnp.where(at < TOK // 2, lens[0, 0], lens[0, 1])
    valid = (at % (TOK // 2)) < count
    src_g[...] = jnp.where(valid, og[...].astype(F32), 0.0).astype(BF16)
    total = row[0:1, :]
    for d in range(1, 16):
        t = lax.rem(z_lo + d // 8, 2) * 8 + mod(x + (d // 2) % 4, 4) * 2 + lax.rem(c + d % 2, 2)
        arrived(sq_all.at[t], r_sq.at[t])
        total = total + sq_all[t]
    factor = lax.rsqrt(total * (1.0 / 4096.0) + 1e-05)
    factor = jnp.transpose(jnp.broadcast_to(factor, (8, TOK)), (1, 0))[:, 0:1]
    src_n[...] = (v * factor * gain[t_me]).astype(BF16)

    everyone(1)
    arrived(bpo, r_po)

    carry = lax.rem(c + z_hi, 2)

    def product(s, first):
        rest = s // 2
        zz = mod(z_hi + carry + rest + 2 * lax.rem(s, 2), 4)

        def wait_rest():
            for dy in range(4):
                j = zz * 4 + dy
                for q in range(6):
                    arrived(wslot(j, q), r_w.at[j, q])

        pl.when(rest == 1)(wait_rest)
        js = pl.ds(zz * 4, 4)
        n = jnp.concatenate([tok[0, zz * 4 + k] for k in range(4)], axis=1)
        g = jnp.concatenate([tok[1, zz * 4 + k] for k in range(4)], axis=1)
        down = jnp.concatenate([bwd[zz * 4 + k] for k in range(4)], axis=1)

        def add(acc, value):
            acc[...] = value if first else acc[...] + value

        add(acc_g, jnp.dot(n, bwg[js].reshape(4 * KB, HID), preferred_element_type=F32))
        add(acc_u, jnp.dot(n, bwu[js].reshape(4 * KB, HID), preferred_element_type=F32))
        cols = pl.ds(pl.multiple_of(zz * (4 * KB), 4 * KB), 4 * KB)
        add(acc_l, lax.dot_general(n, pin[:, cols], (((1,), (1,)), ((), ())), preferred_element_type=F32))
        add(acc_b, lax.dot_general(g, down, (((1,), (1,)), ((), ())), preferred_element_type=F32))

    product(0, True)

    @pl.loop(1, 4)
    def _(s):
        product(s, False)

    acc_o[...] = jnp.zeros_like(acc_o)

    @pl.loop(0, TOK // 128)
    def _(t):
        rows = pl.ds(pl.multiple_of(t * 128, 128), 128)
        gate = acc_g[rows, :]
        sig = 1.0 / (1.0 + jnp.exp(-gate))
        dgate = (acc_b[rows, :] * acc_u[rows, :] * sig * (1.0 + gate * (1.0 - sig))).astype(BF16)
        right = lax.dot_general(
            dgate, bpo[...], (((1,), (1,)), ((), ())), preferred_element_type=F32
        )
        acc_o[...] += lax.dot_general(
            acc_l[rows, :], right, (((0,), (0,)), ((), ())),
            precision=lax.Precision.HIGHEST, preferred_element_type=F32,
        )

    for j in range(NB):
        part[j] = acc_o[4 * j:4 * j + 4, :]

    ph = z_lo + 2 * c
    piece = z_hi * 4 + x
    pair = ph * 4 + y
    me = z_hi * 4 + y
    every_t = [(lax.rem(z_lo + d // 8, 2), mod(x + (d // 2) % 4, 4), lax.rem(c + d % 2, 2)) for d in range(16)]
    last = []

    def send5(src, dst, ssem, rsem, to, stays=None):
        d = pltpu.make_async_remote_copy(
            src_ref=src, dst_ref=dst, send_sem=ssem, recv_sem=rsem, device_id=at5(*to), device_id_type=MESH,
        )
        if stays is None:
            d.start()
            last.append(d.wait_send)
        else:
            def stay():
                pltpu.make_async_copy(src, dst, rsem).start()

            pl.when(jnp.logical_not(stays))(lambda: d.start())
            pl.when(stays)(stay)
            last.append(lambda: pl.when(jnp.logical_not(stays))(lambda: d.wait_send()))

    for n, (zh, xx) in enumerate(team):
        send5(part.at[zh * 4 + xx], got1.at[piece], s1.at[n], r1.at[piece], (zh, y, z_lo, xx, c))
    everyone(0, drain=True)
    everyone(1, drain=True)
    for d in sq_sends:
        d.wait_send()

    def wait_po():
        for d in po_sends:
            d.wait_send()

    pl.when(has_po)(wait_po)
    total = part[piece]
    for zh, xx in team:
        m = zh * 4 + xx
        arrived(got1.at[m], r1.at[m])
        total = total + got1[m]
    mine[...] = total
    for n, (zl, xx, cc) in enumerate(every_t):
        send5(mine, got3.at[pair], s3.at[n], r3.at[pair], (z_hi, x, zl, xx, cc), (x == y) if n == 0 else None)
    for n, (zl, xx, cc) in enumerate(every_t):
        send5(mine, got2.at[piece], s2.at[n], r2.at[piece], (ph, y, zl, xx, cc), (ph == z_hi) if n == 0 else None)
    for p in range(16):
        arrived(got3.at[p], r3.at[p])
    s = jnp.zeros((16, KB), F32)
    for r in range(4):
        f = got3[:, r, :].astype(BF16)
        s = s + lax.dot_general(
            f, q[:, r * RANK:(r + 1) * RANK], (((1,), (1,)), ((), ())), preferred_element_type=F32
        )
    for p in range(16):
        rows4[p] = s[p:p + 1, :]
    for n, (zh, yy) in enumerate(same_t):
        send5(rows4.at[zh * 4 + yy], got4.at[me], s4.at[n], r4.at[me], (zh, yy, z_lo, x, c))
    for p in range(16):
        arrived(got2.at[p], r2.at[p])
        grad[4 * p:4 * p + 4, :] = got2[p]
    total = rows4[me]
    for zh, yy in same_t:
        m = zh * 4 + yy
        arrived(got4.at[m], r4.at[m])
        total = total + got4[m]
    score[...] = total
    for w in last:
        w()


def gathered(li, og, wg, wu, wd, po, pin, gain, lens, q):
    any_ = pl.BlockSpec(memory_space=pl.ANY)
    vmem = pl.BlockSpec(memory_space=pltpu.VMEM)
    smem = pl.BlockSpec(memory_space=pltpu.SMEM)
    dma = pltpu.SemaphoreType.DMA
    piece = pltpu.VMEM((NB, 4, RANK), F32)
    row = pltpu.VMEM((16, 1, KB), F32)
    return pl.pallas_call(
        gather_kernel,
        out_shape=(
            jax.ShapeDtypeStruct((RANK, RANK), F32),
            jax.ShapeDtypeStruct((1, KB), F32),
        ),
        in_specs=[vmem] * 2 + [any_] * 4 + [vmem] * 2 + [smem, vmem],
        out_specs=(vmem, vmem),
        scratch_shapes=[
            pltpu.VMEM((2, NB, TOK, KB), BF16),
            pltpu.VMEM((NB, KB, HID), BF16),
            pltpu.VMEM((NB, KB, HID), BF16),
            pltpu.VMEM((NB, HID, KB), BF16),
            pltpu.VMEM((RANK, HID), BF16),
            pltpu.VMEM((TOK, HID), F32),
            pltpu.VMEM((TOK, HID), F32),
            pltpu.VMEM((TOK, HID), F32),
            pltpu.VMEM((TOK, RANK), F32),
            pltpu.VMEM((RANK, RANK), F32),
            pltpu.VMEM((TOK, KB), BF16),
            pltpu.VMEM((TOK, KB), BF16),
            pltpu.VMEM((1, TOK), F32),
            pltpu.VMEM((16, 1, TOK), F32),
            piece, piece, pltpu.VMEM((4, RANK), F32), piece, piece, row, row,
            dma((2, NB)),
            dma((NB, 6)),
            dma,
            dma((16,)),
            dma((NSEND,)),
            dma((3,)),
            dma((16,)),
            *([dma((16,))] * 8),
        ],
        compiler_params=pltpu.CompilerParams(
            collective_id=0, has_side_effects=True, vmem_limit_bytes=60 << 20
        ),
    )(li, og, wg, wu, wd, po, pin, gain, lens, q)


def on_device(
    layer_input,
    out_grad,
    norm_gain,
    gate_weight,
    up_weight,
    down_weight,
    lengths,
    proj_in,
    proj_out,
    queries,
):
    grad, scores = gathered(
        layer_input.reshape(TOK, KB),
        out_grad.reshape(TOK, KB),
        gate_weight,
        up_weight,
        down_weight,
        proj_out.T,
        proj_in.T,
        norm_gain.reshape(NB, 1, KB),
        lengths,
        queries,
    )
    return (grad.reshape(1, RANK, RANK), scores)


def solution(mesh):
    in_specs = (
        P("dp", None, None, "tensor"),
        P("dp", None, None, "tensor"),
        P(),
        P("dp", "tensor"),
        P("dp", "tensor"),
        P("tensor", "dp"),
        P("dp", None),
        P(),
        P("tensor", None),
        P("tensor", "dp"),
    )
    out_specs = (P("dp", None, None), P("dp", "tensor"))
    return jax.shard_map(
        on_device, mesh=mesh, in_specs=in_specs, out_specs=out_specs, check_vma=False
    )
```

```python
import jax
import jax.numpy as jnp
from jax import lax
from jax.experimental import pallas as pl
from jax.experimental.pallas import tpu as pltpu
from jax.sharding import PartitionSpec as P

MESH = pl.DeviceIdType.MESH
F32 = jnp.float32
BF16 = jnp.bfloat16
TOK = 512
KB = 256
NB = 16
HID = 896
RANK = 64
NSEND = 176

ORDERS = (
    (
        0, 1, 2, 3, 4, 5, 8, 9, 10, 11, 12, 13, 28, 6, 7, 30, 20, 22, 21, 23, 32, 29, 24, 31,
        52, 35, 54, 33, 25, 53, 37, 34, 55, 14, 39, 36, 15, 56, 57, 72, 38, 60, 63, 73, 74, 61, 64, 16,
        26, 40, 41, 62, 42, 27, 65, 44, 58, 43, 17, 59, 45, 47, 18, 66, 75, 67, 49, 69, 68, 19, 46, 51,
        70, 48, 50, 71,
    ),
    (
        0, 1, 2, 3, 4, 5, 8, 6, 7, 9, 28, 10, 30, 29, 11, 31, 12, 32, 35, 33, 60, 37, 13, 20,
        61, 14, 27, 34, 63, 24, 52, 39, 59, 36, 64, 62, 21, 15, 40, 56, 38, 41, 16, 42, 65, 53, 17, 43,
        44, 47, 72, 18, 22, 45, 66, 25, 19, 23, 54, 49, 57, 67, 69, 26, 51, 55, 46, 58, 74, 68, 48, 73,
        70, 50, 75, 71,
    ),
    (
        0, 1, 2, 3, 4, 5, 8, 6, 7, 14, 28, 9, 15, 40, 22, 29, 26, 41, 10, 16, 30, 31, 54, 60,
        23, 42, 27, 43, 58, 11, 17, 33, 35, 55, 45, 32, 18, 66, 12, 47, 59, 44, 20, 19, 21, 73, 13, 49,
        63, 52, 61, 75, 37, 53, 67, 24, 34, 25, 51, 56, 69, 72, 46, 39, 62, 57, 48, 70, 36, 74, 64, 68,
        71, 50, 65, 38,
    ),
    (
        0, 1, 2, 3, 4, 5, 8, 6, 7, 28, 9, 14, 29, 22, 30, 10, 60, 40, 31, 54, 23, 11, 41, 35,
        32, 33, 12, 61, 55, 26, 13, 37, 63, 66, 15, 39, 73, 58, 27, 34, 62, 16, 64, 59, 36, 24, 20, 42,
        43, 38, 17, 44, 65, 75, 56, 47, 25, 18, 21, 45, 19, 52, 67, 57, 49, 53, 69, 46, 51, 68, 74, 72,
        48, 70, 50, 71,
    ),
    (
        0, 1, 2, 3, 4, 5, 8, 6, 7, 28, 9, 22, 29, 10, 30, 54, 60, 31, 23, 32, 11, 26, 33, 35,
        55, 12, 61, 73, 58, 27, 13, 37, 62, 63, 20, 39, 21, 34, 59, 14, 36, 52, 40, 38, 64, 75, 53, 65,
        24, 15, 41, 16, 66, 72, 17, 42, 56, 25, 18, 19, 44, 43, 47, 57, 49, 45, 51, 46, 67, 74, 48, 69,
        50, 70, 68, 71,
    ),
    (
        0, 1, 2, 3, 4, 5, 8, 6, 7, 14, 28, 9, 15, 40, 29, 22, 41, 10, 16, 30, 31, 60, 54, 43,
        42, 23, 11, 33, 17, 45, 35, 12, 26, 32, 55, 47, 66, 18, 44, 13, 73, 27, 58, 37, 63, 19, 24, 61,
        20, 59, 67, 49, 69, 39, 34, 25, 21, 56, 75, 46, 51, 52, 36, 64, 62, 57, 48, 53, 70, 68, 65, 38,
        74, 71, 50, 72,
    ),
    (
        0, 1, 2, 3, 4, 5, 8, 6, 7, 22, 20, 23, 21, 9, 14, 28, 54, 10, 24, 40, 52, 29, 55, 11,
        30, 25, 53, 41, 12, 15, 31, 73, 56, 32, 35, 13, 33, 60, 57, 72, 37, 26, 74, 16, 66, 27, 39, 34,
        43, 42, 58, 61, 63, 59, 36, 64, 17, 45, 62, 44, 47, 75, 38, 65, 18, 19, 67, 69, 49, 46, 51, 68,
        48, 70, 50, 71,
    ),
    (
        0, 1, 2, 3, 4, 5, 8, 9, 10, 11, 12, 13, 28, 6, 7, 30, 32, 29, 31, 35, 33, 37, 34, 39,
        36, 38, 26, 20, 60, 63, 61, 64, 58, 14, 62, 65, 52, 15, 21, 40, 16, 42, 53, 17, 41, 18, 43, 72,
        47, 44, 25, 19, 45, 49, 66, 24, 22, 57, 51, 23, 67, 56, 69, 54, 27, 46, 55, 74, 48, 70, 59, 68,
        73, 71, 50, 75,
    ),
    (
        0, 1, 2, 3, 4, 5, 8, 9, 10, 11, 12, 13, 28, 6, 7, 30, 32, 29, 31, 35, 33, 37, 34, 39,
        36, 38, 60, 63, 22, 25, 61, 64, 54, 62, 65, 14, 23, 15, 57, 40, 16, 42, 41, 17, 55, 26, 43, 18,
        47, 44, 73, 45, 66, 19, 58, 49, 20, 21, 67, 51, 27, 24, 52, 69, 46, 53, 59, 48, 68, 70, 56, 50,
        71, 72, 75, 74,
    ),
    (
        0, 1, 2, 3, 4, 5, 8, 6, 7, 20, 22, 21, 23, 9, 14, 28, 52, 10, 26, 30, 54, 29, 53, 11,
        40, 27, 55, 31, 12, 15, 41, 72, 58, 32, 35, 33, 60, 59, 13, 73, 37, 24, 75, 16, 61, 25, 39, 34,
        43, 42, 56, 63, 66, 36, 57, 64, 17, 45, 62, 18, 44, 47, 38, 65, 74, 49, 19, 67, 46, 69, 51, 48,
        70, 68, 50, 71,
    ),
    (
        0, 1, 2, 3, 4, 5, 8, 6, 7, 14, 28, 9, 15, 40, 29, 20, 41, 10, 16, 30, 31, 60, 52, 43,
        42, 21, 11, 33, 17, 35, 12, 45, 24, 32, 53, 47, 66, 18, 44, 13, 72, 25, 56, 37, 63, 19, 26, 61,
        22, 57, 67, 49, 69, 39, 34, 27, 23, 58, 74, 51, 46, 54, 36, 64, 62, 48, 59, 70, 55, 68, 65, 38,
        75, 71, 50, 73,
    ),
    (
        0, 1, 2, 3, 4, 5, 8, 6, 7, 28, 9, 20, 29, 10, 30, 52, 60, 31, 21, 11, 32, 24, 33, 35,
        53, 12, 61, 72, 56, 25, 13, 37, 34, 63, 22, 39, 23, 62, 57, 14, 36, 54, 40, 38, 64, 74, 55, 65,
        26, 15, 41, 66, 16, 73, 17, 42, 58, 27, 18, 19, 44, 43, 47, 59, 49, 45, 51, 46, 67, 75, 48, 69,
        50, 70, 68, 71,
    ),
    (
        0, 1, 2, 3, 4, 5, 8, 6, 7, 28, 9, 14, 29, 20, 30, 10, 60, 40, 31, 52, 21, 41, 11, 35,
        32, 33, 12, 61, 53, 24, 13, 37, 66, 15, 63, 72, 56, 39, 25, 34, 62, 16, 57, 36, 26, 64, 22, 42,
        38, 17, 43, 44, 74, 58, 65, 27, 18, 23, 47, 19, 54, 45, 49, 67, 59, 55, 46, 51, 68, 75, 69, 73,
        48, 70, 50, 71,
    ),
    (
        0, 1, 2, 3, 4, 5, 8, 6, 7, 14, 28, 9, 15, 40, 20, 29, 24, 41, 10, 16, 30, 31, 52, 60,
        21, 42, 25, 43, 56, 11, 17, 33, 35, 53, 45, 32, 66, 18, 12, 47, 57, 44, 22, 23, 19, 72, 13, 49,
        54, 63, 61, 74, 55, 26, 67, 37, 69, 34, 27, 51, 58, 73, 46, 62, 39, 59, 70, 48, 36, 75, 64, 68,
        71, 50, 65, 38,
    ),
    (
        0, 1, 2, 3, 4, 5, 8, 6, 7, 9, 28, 10, 30, 29, 11, 31, 12, 32, 35, 33, 60, 37, 13, 22,
        24, 14, 61, 34, 63, 54, 39, 56, 36, 64, 23, 62, 15, 27, 40, 38, 41, 55, 16, 42, 65, 59, 43, 26,
        17, 44, 73, 20, 18, 47, 45, 66, 58, 49, 19, 52, 21, 75, 67, 25, 69, 51, 46, 53, 70, 57, 68, 48,
        50, 72, 71, 74,
    ),
    (
        0, 1, 2, 3, 4, 5, 8, 9, 10, 11, 12, 13, 28, 6, 7, 30, 22, 20, 23, 21, 32, 29, 26, 31,
        54, 35, 52, 33, 27, 55, 37, 34, 53, 14, 39, 36, 15, 58, 59, 73, 38, 60, 63, 72, 75, 61, 64, 24,
        40, 41, 62, 16, 42, 25, 65, 56, 43, 17, 57, 44, 45, 66, 47, 18, 74, 49, 67, 69, 46, 19, 68, 70,
        51, 48, 50, 71,
    ),
)


def _steps():
    qs, ns, two = range(6), range(2), range(2)
    steps = [("ws", q) for q in qs] + [("ts", a) for a in two]
    steps += [("wo", n, q) for n in ns for q in qs]
    steps += [("tn", n, cc, a) for n in ns for cc in two for a in two]
    steps += [("wn", n, q, way) for n in ns for q in qs for way in two]
    steps += [("tx", n, cc, a) for n in ns for cc in two for a in two]
    steps += [("wl", n, q) for n in ns for q in qs] + [("tw", n, cc) for n in ns for cc in two]
    return steps


STEPS = _steps()


def mod(a, n):
    return lax.rem(a + 2 * n, n)


def coords():
    dp = lax.axis_index("dp")
    t = lax.axis_index("tensor")
    z_hi, y = dp // 4, lax.rem(dp, 4)
    z_lo, x, c = t // 8, lax.rem(t // 2, 4), lax.rem(t, 2)
    return x, y, 2 * z_hi + z_lo, c


def device(x, y, z, c):
    if isinstance(z, int):
        return ((z // 2) * 4 + y, (z % 2) * 8 + x * 2 + c)
    return ((z // 2) * 4 + y, lax.rem(z, 2) * 8 + x * 2 + c)


def at5(zh, yy, zl, xx, cc):
    return (zh * 4 + yy, zl * 8 + xx * 2 + cc)


def carried(z, c):
    z_hi, z_lo = z // 2, z % 2
    s = (c + z_hi) % 2
    zs = ((z_hi + s) % 4, (z_hi + s + 2) % 4)
    return zs[::-1] if s and z_lo == 0 else zs


def gather_kernel(
    li, og, wg, wu, wd, po, pin, gain, lens, q,
    grad, score,
    tok, bwg, bwu, bwd, bpo, acc_g, acc_u, acc_b, acc_l, acc_o, src_n, src_g, sq_mine, sq_all,
    part, got1, mine, got2, got3, got4, rows4,
    r_tok, r_w, r_po, r_sq, s_all, s_po, s_sq, r1, r2, r3, r4, s1, s2, s3, s4,
):
    x, y, z, c = coords()
    z_hi, z_lo = z // 2, lax.rem(z, 2)
    xp, xm, yp, ym = mod(x + 1, 4), mod(x - 1, 4), mod(y + 1, 4), mod(y - 1, 4)
    other = (x, y, z, 1 - c)
    z1 = mod(z + 1 - 2 * z_lo, 8)
    ka, kc = lax.rem(z_hi, 2), z_hi // 2

    barrier = pltpu.get_barrier_semaphore()
    peers = [(x, yp, z, c), (x, ym, z, c), other]
    for dz in range(1, 8):
        for cc in (0, 1):
            peers.append((x, y, mod(z + dz, 8), cc))
    for dx in range(1, 4):
        for zz in (z, z1):
            for cc in (0, 1):
                peers.append((mod(x + dx, 4), y, zz, cc))
    team = [(mod(z_hi + d // 4, 4), mod(x + d % 4, 4)) for d in range(1, 16)]
    same_t = [(mod(z_hi + d // 4, 4), mod(y + d % 4, 4)) for d in range(1, 16)]
    ends = [(zh, y, z_lo, xx, c) for d, (zh, xx) in enumerate(team, 1) if d > 3 and d % 4]
    ends += [(zh, yy, z_lo, x, c) for d, (zh, yy) in enumerate(same_t, 1) if d % 4 and d not in (1, 3)]
    for d in range(16):
        ends.append((d // 4, y, lax.rem(z_hi, 2), d % 4, z_hi // 2))
        ends.append((z_hi, d // 4, d % 2, y, (d // 2) % 2))
    signals = [device(*p) for p in peers] + [at5(*p) for p in ends]
    for p in signals:
        pl.semaphore_signal(barrier, inc=1, device_id=p, device_id_type=MESH)
    pl.semaphore_wait(barrier, len(signals))

    def remote(src, dst, ssem, rsem, to):
        return pltpu.make_async_remote_copy(
            src_ref=src, dst_ref=dst, send_sem=ssem, recv_sem=rsem,
            device_id=device(*to), device_id_type=MESH,
        )

    def arrived(ref, sem):
        pltpu.make_async_copy(ref, ref, sem).wait()

    chunks = [(0, 0), (1, 0), (2, 0), (0, 1), (1, 1), (2, 1)]

    def lanes(j):
        return pl.ds(pl.multiple_of(lax.rem(j, 4) * KB, KB), KB)

    def wslot(j, q):
        m, h = chunks[q]
        if m == 2:
            return bwd.at[j // 4, pl.ds(h * (HID // 2), HID // 2), lanes(j)]
        return (bwg, bwu)[m].at[j, pl.ds(h * (KB // 2), KB // 2)]

    def tslot(a, j):
        return tok.at[a, j // 4, :, lanes(j)]

    def wsrc(q):
        m, h = chunks[q]
        n = KB // 2 if m < 2 else HID // 2
        return (wg, wu, wd)[m].at[pl.ds(h * n, n)]

    def walk(z, c, numbers, first, drain):
        z_hi, z_lo = z // 2, z % 2
        ka, z1 = z_hi % 2, z ^ 1
        zs = carried(z, c)
        kt = z_lo + 2 * c
        rel, f = (z_hi - kt) % 4, z_hi % 2
        entry = 1 if rel == 1 else 0 if rel == 3 else 1 - z_lo
        far = z1 if rel == 0 else 2 * kt + entry
        b, i = z_hi % 2, z_hi // 2
        hop = 2 if z_lo == b else 1
        r0 = (z - 2 * z_lo - 4 * c) % 8
        u0 = 1 - ((r0 + 7) % 8) // 4
        us = (u0, 1 - u0)
        count = [first]

        def send(src, dst, rsem, to):
            d = remote(src, dst, s_all.at[count[0]], rsem, to)
            count[0] += 1
            d.wait_send() if drain else d.start()

        def await_(ref, sem):
            if not drain:
                arrived(ref, sem)

        for number in numbers:
            kind, *arg = STEPS[number]
            if kind == "ws":
                j, q = z_hi * 4 + y, arg[0]
                if rel == 0 and f != c:
                    send(wsrc(q), wslot(j, q), r_w.at[j, q], (x, y, z, 1 - c))
                if rel == 0 and f == c and not drain:
                    pltpu.make_async_copy(wsrc(q), wslot(j, q), r_w.at[j, q]).start()
                send(wsrc(q), wslot(j, q), r_w.at[j, q], (x, y, far, f))
            elif kind == "ts":
                a = arg[0]
                j = z_lo * 8 + x * 2 + c
                src, dst, sem = (src_n, src_g)[a], tslot(a, j), r_tok.at[a, j]
                if hop == 2 and i != c:
                    send(src, dst, sem, (x, y, z, i))
                if hop == 2 and i == c and not drain:
                    pltpu.make_async_copy(src, dst, sem).start()
                send(src, dst, sem, (x, y, (z + hop) % 8, i))
                send(src, dst, sem, (x, y, (z - hop) % 8, i))
            elif kind == "wo":
                n, q = arg
                j, r = zs[n] * 4 + y, (zs[n] - z_hi) % 4
                ent = 1 if r == 1 else 0 if r == 3 else 1 - ka
                blk, sem = wslot(j, q), r_w.at[j, q]
                await_(blk, sem)
                if r != 0 and z_lo == ent:
                    send(blk, blk, sem, (x, y, z1, c))
                send(blk, blk, sem, (x, yp, z, c))
                send(blk, blk, sem, (x, ym, z, c))
                send(blk, blk, sem, (x, y, z, 1 - c))
            elif kind == "wn":
                n, q, way = arg
                j = zs[n] * 4 + (ym, yp)[way]
                blk, sem = wslot(j, q), r_w.at[j, q]
                await_(blk, sem)
                if q // 3 == way:
                    send(blk, blk, sem, (x, (yp, ym)[way], z, c))
                send(blk, blk, sem, (x, y, z, 1 - c))
            elif kind == "wl":
                n, q = arg
                j = zs[n] * 4 + mod(y + 2, 4)
                blk, sem = wslot(j, q), r_w.at[j, q]
                await_(blk, sem)
                send(blk, blk, sem, (x, y, z, 1 - c))
            elif kind == "tn":
                n, cc, a = arg
                u = us[n]
                r = (r0 - u) % 8
                j = u * 8 + x * 2 + cc
                blk, sem = tslot(a, j), r_tok.at[a, j]
                await_(blk, sem)
                if r in ((1, 2), (1,))[a]:
                    send(blk, blk, sem, (x, y, (z + 2) % 8, c))
                if r in ((7,), (6, 7))[a]:
                    send(blk, blk, sem, (x, y, (z - 2) % 8, c))
                send(blk, blk, sem, (xp, y, z, c))
                send(blk, blk, sem, (xm, y, z, c))
            elif kind == "tx":
                n, cc, a = arg
                j = us[n] * 8 + (xm, xp)[a] * 2 + cc
                blk, sem = tslot(a, j), r_tok.at[a, j]
                await_(blk, sem)
                send(blk, blk, sem, ((xp, xm)[a], y, z, c))
            elif kind == "tw":
                n, cc = arg
                for a in (0, 1):
                    for xx in ((xp, xm)[a], mod(x + 2, 4)):
                        j = us[n] * 8 + xx * 2 + cc
                        await_(tslot(a, j), r_tok.at[a, j])
        return count[0]

    sent = {}

    def everyone(part, drain=False):
        for zz in range(8):
            for cc in range(2):
                order = ORDERS[zz * 2 + cc]
                cut = min(order.index(n) for n, s in enumerate(STEPS) if s[0] == "ts")
                numbers = (order[:cut], order[cut:])[part]
                first = sent[zz, cc] if part else 0

                def go(zz=zz, cc=cc, numbers=numbers, first=first):
                    sent[zz, cc] = walk(zz, cc, numbers, first, drain)

                pl.when((z == zz) & (c == cc))(go)

    v = li[...].astype(F32)
    ones = jnp.ones((8, KB), F32)
    row = lax.dot_general(
        ones, v * v, (((1,), (1,)), ((), ())), precision=lax.Precision.HIGHEST, preferred_element_type=F32
    )
    sq_mine[...] = row[0:1, :]
    t_me = z_lo * 8 + x * 2 + c
    sq_sends = []
    for d in range(1, 16):
        to = (mod(x + (d // 2) % 4, 4), y, (z, z1)[d // 8], lax.rem(c + d % 2, 2))
        sq_sends.append(remote(sq_mine, sq_all.at[t_me], s_sq.at[d], r_sq.at[t_me], to))
        sq_sends[-1].start()
    everyone(0)

    has_po = (z_lo == ka) & (c == kc)
    po_sends = [
        remote(po, bpo, s_po.at[0], r_po, other),
        remote(po, bpo, s_po.at[1], r_po, (x, y, z1, 0)),
        remote(po, bpo, s_po.at[2], r_po, (x, y, z1, 1)),
    ]

    def start_po():
        for d in po_sends:
            d.start()
        pltpu.make_async_copy(po, bpo, r_po).start()

    pl.when(has_po)(start_po)

    at = lax.broadcasted_iota(jnp.int32, (TOK, KB), 0)
    count = jnp.where(at < TOK // 2, lens[0, 0], lens[0, 1])
    valid = (at % (TOK // 2)) < count
    src_g[...] = jnp.where(valid, og[...].astype(F32), 0.0).astype(BF16)
    total = row[0:1, :]
    for d in range(1, 16):
        t = lax.rem(z_lo + d // 8, 2) * 8 + mod(x + (d // 2) % 4, 4) * 2 + lax.rem(c + d % 2, 2)
        arrived(sq_all.at[t], r_sq.at[t])
        total = total + sq_all[t]
    factor = lax.rsqrt(total * (1.0 / 4096.0) + 1e-05)
    factor = jnp.transpose(jnp.broadcast_to(factor, (8, TOK)), (1, 0))[:, 0:1]
    src_n[...] = (v * factor * gain[t_me]).astype(BF16)

    everyone(1)
    arrived(bpo, r_po)

    carry = lax.rem(c + z_hi, 2)

    def product(s, first):
        rest = s // 2
        zz = mod(z_hi + carry + rest + 2 * lax.rem(s, 2), 4)

        def wait_rest():
            for dy in range(4):
                j = zz * 4 + dy
                for q in range(6):
                    arrived(wslot(j, q), r_w.at[j, q])

        pl.when(rest == 1)(wait_rest)
        js = pl.ds(zz * 4, 4)
        def add(acc, value):
            acc[...] = value if first else acc[...] + value

        n = tok[0, zz]
        add(acc_g, jnp.dot(n, bwg[js].reshape(4 * KB, HID), preferred_element_type=F32))
        add(acc_u, jnp.dot(n, bwu[js].reshape(4 * KB, HID), preferred_element_type=F32))
        cols = pl.ds(pl.multiple_of(zz * (4 * KB), 4 * KB), 4 * KB)
        add(acc_l, lax.dot_general(n, pin[:, cols], (((1,), (1,)), ((), ())), preferred_element_type=F32))
        add(acc_b, lax.dot_general(tok[1, zz], bwd[zz], (((1,), (1,)), ((), ())), preferred_element_type=F32))

    product(0, True)

    @pl.loop(1, 4)
    def _(s):
        product(s, False)

    acc_o[...] = jnp.zeros_like(acc_o)

    @pl.loop(0, TOK // 128)
    def _(t):
        rows = pl.ds(pl.multiple_of(t * 128, 128), 128)
        gate = acc_g[rows, :]
        sig = 1.0 / (1.0 + jnp.exp(-gate))
        dgate = (acc_b[rows, :] * acc_u[rows, :] * sig * (1.0 + gate * (1.0 - sig))).astype(BF16)
        right = lax.dot_general(
            dgate, bpo[...], (((1,), (1,)), ((), ())), preferred_element_type=F32
        )
        acc_o[...] += lax.dot_general(
            acc_l[rows, :], right, (((0,), (0,)), ((), ())),
            precision=lax.Precision.HIGHEST, preferred_element_type=F32,
        )

    for j in range(NB):
        part[j] = acc_o[4 * j:4 * j + 4, :]

    ph = z_lo + 2 * c
    piece = z_hi * 4 + x
    pair = ph * 4 + y
    me = z_hi * 4 + y
    every_t = [(lax.rem(z_lo + d // 8, 2), mod(x + (d // 2) % 4, 4), lax.rem(c + d % 2, 2)) for d in range(16)]
    last = []

    def send5(src, dst, ssem, rsem, to, stays=None):
        d = pltpu.make_async_remote_copy(
            src_ref=src, dst_ref=dst, send_sem=ssem, recv_sem=rsem, device_id=at5(*to), device_id_type=MESH,
        )
        if stays is None:
            d.start()
            last.append(d.wait_send)
        else:
            def stay():
                pltpu.make_async_copy(src, dst, rsem).start()

            pl.when(jnp.logical_not(stays))(lambda: d.start())
            pl.when(stays)(stay)
            last.append(lambda: pl.when(jnp.logical_not(stays))(lambda: d.wait_send()))

    for n, (zh, xx) in enumerate(team):
        send5(part.at[zh * 4 + xx], got1.at[piece], s1.at[n], r1.at[piece], (zh, y, z_lo, xx, c))
    everyone(0, drain=True)
    everyone(1, drain=True)
    for d in sq_sends:
        d.wait_send()

    def wait_po():
        for d in po_sends:
            d.wait_send()

    pl.when(has_po)(wait_po)
    total = part[piece]
    for zh, xx in team:
        m = zh * 4 + xx
        arrived(got1.at[m], r1.at[m])
        total = total + got1[m]
    mine[...] = total
    for n, (zl, xx, cc) in enumerate(every_t):
        send5(mine, got3.at[pair], s3.at[n], r3.at[pair], (z_hi, x, zl, xx, cc), (x == y) if n == 0 else None)
    for n, (zl, xx, cc) in enumerate(every_t):
        send5(mine, got2.at[piece], s2.at[n], r2.at[piece], (ph, y, zl, xx, cc), (ph == z_hi) if n == 0 else None)
    for p in range(16):
        arrived(got3.at[p], r3.at[p])
    s = jnp.zeros((16, KB), F32)
    for r in range(4):
        f = got3[:, r, :].astype(BF16)
        s = s + lax.dot_general(
            f, q[:, r * RANK:(r + 1) * RANK], (((1,), (1,)), ((), ())), preferred_element_type=F32
        )
    for p in range(16):
        rows4[p] = s[p:p + 1, :]
    for n, (zh, yy) in enumerate(same_t):
        send5(rows4.at[zh * 4 + yy], got4.at[me], s4.at[n], r4.at[me], (zh, yy, z_lo, x, c))
    for p in range(16):
        arrived(got2.at[p], r2.at[p])
        grad[4 * p:4 * p + 4, :] = got2[p]
    total = rows4[me]
    for zh, yy in same_t:
        m = zh * 4 + yy
        arrived(got4.at[m], r4.at[m])
        total = total + got4[m]
    score[...] = total
    for w in last:
        w()


def gathered(li, og, wg, wu, wd, po, pin, gain, lens, q):
    any_ = pl.BlockSpec(memory_space=pl.ANY)
    vmem = pl.BlockSpec(memory_space=pltpu.VMEM)
    smem = pl.BlockSpec(memory_space=pltpu.SMEM)
    dma = pltpu.SemaphoreType.DMA
    piece = pltpu.VMEM((NB, 4, RANK), F32)
    row = pltpu.VMEM((16, 1, KB), F32)
    return pl.pallas_call(
        gather_kernel,
        out_shape=(
            jax.ShapeDtypeStruct((RANK, RANK), F32),
            jax.ShapeDtypeStruct((1, KB), F32),
        ),
        in_specs=[vmem] * 2 + [any_] * 4 + [vmem] * 2 + [smem, vmem],
        out_specs=(vmem, vmem),
        scratch_shapes=[
            pltpu.VMEM((2, NB // 4, TOK, 4 * KB), BF16),
            pltpu.VMEM((NB, KB, HID), BF16),
            pltpu.VMEM((NB, KB, HID), BF16),
            pltpu.VMEM((NB // 4, HID, 4 * KB), BF16),
            pltpu.VMEM((RANK, HID), BF16),
            pltpu.VMEM((TOK, HID), F32),
            pltpu.VMEM((TOK, HID), F32),
            pltpu.VMEM((TOK, HID), F32),
            pltpu.VMEM((TOK, RANK), F32),
            pltpu.VMEM((RANK, RANK), F32),
            pltpu.VMEM((TOK, KB), BF16),
            pltpu.VMEM((TOK, KB), BF16),
            pltpu.VMEM((1, TOK), F32),
            pltpu.VMEM((16, 1, TOK), F32),
            piece, piece, pltpu.VMEM((4, RANK), F32), piece, piece, row, row,
            dma((2, NB)),
            dma((NB, 6)),
            dma,
            dma((16,)),
            dma((NSEND,)),
            dma((3,)),
            dma((16,)),
            *([dma((16,))] * 8),
        ],
        compiler_params=pltpu.CompilerParams(
            collective_id=0, has_side_effects=True, vmem_limit_bytes=60 << 20
        ),
    )(li, og, wg, wu, wd, po, pin, gain, lens, q)


def on_device(
    layer_input,
    out_grad,
    norm_gain,
    gate_weight,
    up_weight,
    down_weight,
    lengths,
    proj_in,
    proj_out,
    queries,
):
    grad, scores = gathered(
        layer_input.reshape(TOK, KB),
        out_grad.reshape(TOK, KB),
        gate_weight,
        up_weight,
        down_weight,
        proj_out.T,
        proj_in.T,
        norm_gain.reshape(NB, 1, KB),
        lengths,
        queries,
    )
    return (grad.reshape(1, RANK, RANK), scores)


def solution(mesh):
    in_specs = (
        P("dp", None, None, "tensor"),
        P("dp", None, None, "tensor"),
        P(),
        P("dp", "tensor"),
        P("dp", "tensor"),
        P("tensor", "dp"),
        P("dp", None),
        P(),
        P("tensor", None),
        P("tensor", "dp"),
    )
    out_specs = (P("dp", None, None), P("dp", "tensor"))
    return jax.shard_map(
        on_device, mesh=mesh, in_specs=in_specs, out_specs=out_specs, check_vma=False
    )
```
